512 devices in a mesh: seq: 64 (over y, z), tensor: 8 (over x, core).
Axes of the slice: x: 4, y: 4, z: 16, core: 2. Of those that a mesh axis runs over, the one named last changes fastest.
Arguments:
- queries: bfloat16 [8192, 8192], P('seq', 'tensor'), may hold values from -360 to 360
- hidden: bfloat16 [8192, 8192], P('seq', 'tensor'), may hold values from -6 to 6
- key_value_weight: bfloat16 [2, 8192, 1024], P(None, 'tensor', 'seq'), may hold values from -0.0625 to 0.0625
- key_value_bias: bfloat16 [2, 1024], P(None, 'tensor'), may hold values from -3 to 3
- positions: int32 [3, 8192], P(None, 'seq'), may hold values from 0 to 78, as said below
- sink_index: int32 [512], replicated, may hold values from 0 to 8191, as said below
Outputs:
- attended: bfloat16 [8192, 8192], P('seq', 'tensor')
The draws below stay inside these ranges and needn't reach their ends.
Inputs may be any that keep to these rules, and one draw needn't show every extreme that they name: `positions`: rows are the temporal, height and width ids; tokens come in frames of 16 x 16; within a frame the temporal id is fixed, and the height and width ids are the temporal id plus the token's row and column in the frame. `sink_index`: 512 distinct token indices in increasing order, 0 and 8191 among them.
All inputs are finite; a program needn't handle non-finite values.
Results may differ from the reference program's by a relative error of at most 0.012.
The reference program's roundings to bfloat16 on the way count: a program that leaves them out, or rounds other values in their place, can miss the bound.
Values may be sent and summed in bfloat16 or wider, within the bound.
A program may use at most 128 MiB of HBM per device.

```python
import math
import jax
import jax.numpy as jnp
from jax import lax

D = 8192
H = 64
KVH = 8
HD = 128
W = 4096
NSINK = 512
GRID = 16
TQ = 128
TOKENS = 8192


def draw_queries(key, part):
    key = jax.random.fold_in(key, 11)
    normal_key = jax.random.fold_in(key, 0)
    base = jnp.clip(jax.random.normal(normal_key, (TOKENS, H * HD), jnp.float32), -6.0, 6.0) * 2.5
    return base.astype(jnp.bfloat16)


def draw_positions(key, part):
    key = jax.random.fold_in(key, 12)
    frames = TOKENS // (GRID * GRID)
    extra = jax.random.randint(key, (frames,), 0, 2).astype(jnp.int32)
    extra = extra.at[frames - 1].set(1)
    frame_time = 2 * jnp.arange(frames, dtype=jnp.int32) + extra
    token_index = jnp.arange(TOKENS, dtype=jnp.int32)
    frame_index = token_index // (GRID * GRID)
    inside = token_index % (GRID * GRID)
    temporal = frame_time[frame_index]
    height = temporal + inside // GRID
    width_ids = temporal + inside % GRID
    return jnp.stack([temporal, height, width_ids], axis=0).astype(jnp.int32)


def draw_sink_index(key, part):
    key = jax.random.fold_in(key, 13)
    middle = jax.random.permutation(key, TOKENS - 2)[:NSINK - 2].astype(jnp.int32) + 1
    whole = jnp.concatenate([jnp.zeros((1,), jnp.int32), middle, jnp.full((1,), TOKENS - 1, jnp.int32)])
    return jnp.sort(whole).astype(jnp.int32)


def shard_levels(key, extent, cuts, least, largest):
    def one(dim, shards_of):
        heights = jax.random.uniform(jax.random.fold_in(jax.random.fold_in(key, 6), dim), (shards_of,), jnp.float32, least / len(cuts), largest / len(cuts))
        return jnp.repeat(jnp.exp(heights), extent[dim] // shards_of).reshape((-1,) + (1,) * (len(extent) - dim - 1))

    level = one(*cuts[0])
    for cut in cuts[1:]:
        level = level * one(*cut)
    return level


def bell_draw(key, extent, deviation, reach, pieces=(), kind=jnp.bfloat16):
    result = jax.random.normal(key, extent, jnp.float32) * deviation
    if len(pieces) > 0:
        result = shard_levels(key, extent, pieces, -0.22, 0.18) * result
    return jnp.clip(result, min=-reach, max=reach).astype(kind)


def setup_inputs(seed: int = 0) -> dict:
    splits = jax.random.split(jax.random.key(seed), 7)
    queries = draw_queries(jax.random.fold_in(splits[6], 71), 0)
    hidden = bell_draw(splits[1], (TOKENS, D), 1.0, 6.0, ((0, 64), (1, 8)))
    key_value_weight = bell_draw(splits[2], (2, D, KVH * HD), D ** -0.5, 0.0625, ((1, 8), (2, 64)))
    key_value_bias = bell_draw(splits[3], (2, KVH * HD), 0.5, 3.0, ((1, 8),))
    positions = draw_positions(jax.random.fold_in(splits[6], 71), 0)
    sink_index = draw_sink_index(jax.random.fold_in(splits[6], 71), 0)
    return dict(queries=queries, hidden=hidden, key_value_weight=key_value_weight, key_value_bias=key_value_bias, positions=positions, sink_index=sink_index)


def rope_tables(positions):
    half_width = HD // 2
    pair_index = jnp.arange(half_width, dtype=jnp.int32)
    inverse = jnp.exp(pair_index.astype(jnp.float32) * (-2.0 * math.log(1000000.0) / HD))
    first_cut = HD // 8
    second = first_cut + 3 * HD // 16
    chosen = jnp.where(pair_index[None, :] < first_cut, positions[0][:, None],
                       jnp.where(pair_index[None, :] < second, positions[1][:, None], positions[2][:, None]))
    angles = chosen.astype(jnp.float32) * inverse[None, :]
    angles = jnp.concatenate([angles, angles], axis=1)
    return jnp.cos(angles), jnp.sin(angles)


def rotate(vectors, cosine_table, sine_table):
    half_width = HD // 2
    turned = jnp.concatenate([-vectors[..., half_width:], vectors[..., :half_width]], axis=-1)
    return vectors * cosine_table[:, None, :] + turned * sine_table[:, None, :]


def reference(queries, hidden, key_value_weight, key_value_bias, positions, sink_index):
    cosine_table, sine_table = rope_tables(positions)
    keys_raw = jnp.dot(hidden, key_value_weight[0], preferred_element_type=jnp.float32) + key_value_bias[0].astype(jnp.float32)
    values_raw = jnp.dot(hidden, key_value_weight[1], preferred_element_type=jnp.float32) + key_value_bias[1].astype(jnp.float32)
    rotated_keys = rotate(keys_raw.reshape(TOKENS, KVH, HD), cosine_table, sine_table).astype(jnp.bfloat16)
    values = values_raw.reshape(TOKENS, KVH, HD).astype(jnp.bfloat16)
    rotated_queries = rotate(queries.astype(jnp.float32).reshape(TOKENS, H, HD), cosine_table, sine_table).astype(jnp.bfloat16)
    group_size = H // KVH
    sink_keys = rotated_keys[sink_index].astype(jnp.float32)
    sink_values = values[sink_index].astype(jnp.float32)
    padded_keys = jnp.concatenate([jnp.zeros((W, KVH, HD), jnp.bfloat16), rotated_keys], axis=0)
    padded_values = jnp.concatenate([jnp.zeros((W, KVH, HD), jnp.bfloat16), values], axis=0)
    scale = HD ** -0.5

    def one_block(block_number):
        first_row = block_number * TQ
        query_block = lax.dynamic_slice_in_dim(rotated_queries, first_row, TQ, 0).astype(jnp.float32).reshape(TQ, KVH, group_size, HD)
        key_block = lax.dynamic_slice_in_dim(padded_keys, first_row, W + TQ, 0).astype(jnp.float32)
        value_block = lax.dynamic_slice_in_dim(padded_values, first_row, W + TQ, 0).astype(jnp.float32)
        query_pos = first_row + jnp.arange(TQ, dtype=jnp.int32)
        key_pos = first_row - W + jnp.arange(W + TQ, dtype=jnp.int32)
        window_ok = (key_pos[None, :] <= query_pos[:, None]) & (key_pos[None, :] > query_pos[:, None] - W) & (key_pos[None, :] >= 0)
        sink_ok = sink_index[None, :] <= query_pos[:, None] - W
        window_scores = jnp.einsum('tkgd,lkd->kgtl', query_block, key_block) * scale
        sink_scores = jnp.einsum('tkgd,nkd->kgtn', query_block, sink_keys) * scale
        window_scores = jnp.where(window_ok[None, None], window_scores, -1e30)
        sink_scores = jnp.where(sink_ok[None, None], sink_scores, -1e30)
        running_max = jnp.maximum(window_scores.max(-1), sink_scores.max(-1))
        window_exp = jnp.exp(window_scores - running_max[..., None])
        sink_exp = jnp.exp(sink_scores - running_max[..., None])
        running_sum = window_exp.sum(-1) + sink_exp.sum(-1)
        window_weights = window_exp.astype(jnp.bfloat16).astype(jnp.float32)
        sink_weights = sink_exp.astype(jnp.bfloat16).astype(jnp.float32)
        mixed = jnp.einsum('kgtl,lkd->tkgd', window_weights, value_block) + jnp.einsum('kgtn,nkd->tkgd', sink_weights, sink_values)
        normalized = mixed / jnp.transpose(running_sum, (2, 0, 1))[..., None]
        return normalized.reshape(TQ, H * HD).astype(jnp.bfloat16)

    blocks = lax.map(one_block, jnp.arange(TOKENS // TQ, dtype=jnp.int32))
    return blocks.reshape(TOKENS, H * HD)
```

```python
import functools
import math

import jax
import jax.numpy as jnp
from jax import lax
from jax.experimental import pallas as pl
from jax.experimental.pallas import tpu as pltpu
from jax.sharding import PartitionSpec as P

H = 64
KVH = 8
HD = 128
W = 4096
NX = 4
NY = 4
NZ = 16
NS = NY * NZ
TQ = 128
G = H // KVH
DL = 1024
NSINK = 512
MESH = pl.DeviceIdType.MESH
LOG2E = 1.4426950408889634
BF = jnp.bfloat16
F32 = jnp.float32


def coords():
    s = lax.axis_index("seq")
    t = lax.axis_index("tensor")
    return s, t, t // 2, t % 2, s // NZ, s % NZ


def remote(src, dst, send, recv, seq, tensor):
    return pltpu.make_async_remote_copy(
        src_ref=src,
        dst_ref=dst,
        send_sem=send,
        recv_sem=recv,
        device_id=(seq, tensor),
        device_id_type=MESH,
    )


def nt_dot(a, b):
    return lax.dot_general(a, b, (((1,), (1,)), ((), ())), preferred_element_type=F32)


def rope_tables(p_ref):
    row = lax.broadcasted_iota(jnp.int32, (HD, TQ), 0)
    pair = lax.rem(row, HD // 2)
    inverse = jnp.exp(pair.astype(F32) * (-2.0 * math.log(1000000.0) / HD))
    first = HD // 8
    second = first + 3 * HD // 16
    pos = p_ref[...]
    chosen = jnp.where(
        pair < first,
        jnp.broadcast_to(pos[0:1], (HD, TQ)),
        jnp.where(
            pair < second,
            jnp.broadcast_to(pos[1:2], (HD, TQ)),
            jnp.broadcast_to(pos[2:3], (HD, TQ)),
        ),
    )
    angles = chosen.astype(F32) * inverse
    cosine = jnp.cos(angles)
    sine = jnp.where(row < HD // 2, -jnp.sin(angles), jnp.sin(angles))
    return jnp.transpose(cosine), jnp.transpose(sine)


def rotate(u, cosine, sine):
    return u * cosine + pltpu.roll(u, HD // 2, 1) * sine


def project(
    q_ref, h_ref, w_ref, b_ref, p_ref, qo_ref, ko_ref, vo_ref,
    hid, wbuf, p3s, p3r, p4s, p4r, cos_ref, sin_ref,
    hs, hr, fs, fr, bs, br, p3ss, p3rs, p4ss, p4rs,
):
    s, t, x, c, y, z = coords()
    up, down = y * NZ + lax.rem(z + 1, NZ), y * NZ + lax.rem(z + NZ - 1, NZ)
    other = x * 2 + (1 - c)
    mine = x == y

    barrier = pltpu.get_barrier_semaphore()

    def greet(seq, tensor):
        pl.semaphore_signal(barrier, inc=1, device_id=(seq, tensor), device_id_type=MESH)

    greet(s, other)
    greet(up, t)
    greet(down, t)
    for d in range(1, NY):
        greet(lax.rem(y + d, NY) * NZ + z, t)
    for xs in range(NX):
        @pl.when(jnp.logical_not(mine & (x == xs)))
        def _(xs=xs):
            greet(x * NZ + z, xs * 2 + c)

    def w_rows(origin, kv):
        return wbuf.at[origin // 8, pl.ds(pl.multiple_of(kv * HD + lax.rem(origin, 8) * 16, 16), 16)]

    for kv in range(2):
        w_rows(z, kv)[...] = w_ref[kv]
    hid[y] = h_ref[...]
    pl.semaphore_wait(barrier, jnp.where(mine, 9, 10))

    def h_copy(d):
        return remote(h_ref, hid.at[y], hs.at[d], hr.at[d], lax.rem(y + d, NY) * NZ + z, t)

    def f_copy(k, kv):
        rows = w_rows(lax.rem(z - (k - 1) + NZ, NZ), kv)
        return remote(rows, rows, fs.at[k, kv], fr.at[k, kv], up, t)

    def b_copy(k, kv):
        rows = w_rows(lax.rem(z + (k - 1), NZ), kv)
        return remote(rows, rows, bs.at[k, kv], br.at[k, kv], down, t)

    def f_wait(k, kv):
        rows = w_rows(lax.rem(z - k + NZ, NZ), kv)
        remote(rows, rows, fs.at[k, kv], fr.at[k, kv], up, t).wait_recv()

    def b_wait(k, kv):
        rows = w_rows(lax.rem(z + k, NZ), kv)
        remote(rows, rows, bs.at[k, kv], br.at[k, kv], down, t).wait_recv()

    for kv in range(2):
        f_copy(1, kv).start()
        b_copy(1, kv).start()
    for d in (1, 3, 2):
        h_copy(d).start()

    cosine, sine = rope_tables(p_ref)
    cos_ref[...] = cosine
    sin_ref[...] = sine
    for k in range(2, 9):
        for kv in range(2):
            f_wait(k - 1, kv)
            f_copy(k, kv).start()
            b_wait(k - 1, kv)
            if k <= 7:
                b_copy(k, kv).start()
        for g in ([k - 2] if k < 8 else [6, 7]):
            u = q_ref[:, g * HD : (g + 1) * HD].astype(F32)
            qo_ref[g * TQ : (g + 1) * TQ, :] = rotate(u, cos_ref[...], sin_ref[...]).astype(BF)
    for d in range(1, NY):
        slot = hid.at[lax.rem(y + NY - d, NY)]
        remote(slot, slot, hs.at[d], hr.at[d], s, t).wait_recv()
    for kv in range(2):
        f_wait(8, kv)

    for i in range(NY):
        p3s[i] = nt_dot(hid[i], wbuf[1 - c])
        remote(p3s.at[i], p3r.at[i], p3ss.at[i], p3rs.at[i], s, other).start()
    for i in range(NY):
        p4s[i] = nt_dot(hid[i], wbuf[c])

    def p4_copy(i):
        return remote(p4s.at[i], p4r.at[x], p4ss.at[i], p4rs.at[x], i * NZ + z, y * 2 + c)

    for i in range(NY):
        remote(p3s.at[i], p3r.at[i], p3ss.at[i], p3rs.at[i], s, other).wait_recv()
        p4s[i] += p3r[i]

        @pl.when(mine & (y == i))
        def _(i=i):
            p4r[x] = p4s[i]

        @pl.when(jnp.logical_not(mine & (y == i)))
        def _(i=i):
            p4_copy(i).start()

    for xs in range(NX):
        @pl.when(jnp.logical_not(mine & (x == xs)))
        def _(xs=xs):
            remote(p4r.at[xs], p4r.at[xs], p4ss.at[xs], p4rs.at[xs], s, t).wait_recv()

    total = (p4r[0] + p4r[1]) + (p4r[2] + p4r[3])
    keys = total[:, :HD] + b_ref[0:1].astype(F32)
    ko_ref[...] = rotate(keys, cos_ref[...], sin_ref[...]).astype(BF)
    vo_ref[...] = (total[:, HD:] + b_ref[1:2].astype(F32)).astype(BF)

    for d in range(1, NY):
        h_copy(d).wait_send()
    for k in range(1, 9):
        for kv in range(2):
            f_copy(k, kv).wait_send()
            if k <= 7:
                b_copy(k, kv).wait_send()
    for i in range(NY):
        remote(p3s.at[i], p3r.at[i], p3ss.at[i], p3rs.at[i], s, other).wait_send()

        @pl.when(jnp.logical_not(mine & (y == i)))
        def _(i=i):
            p4_copy(i).wait_send()


def rounds():
    table = []
    for k in range(1, 9):
        waits = []
        back = 17 - k
        if k == 8:
            waits.append((32, [(-1, 31)]))
        if back > 8:
            waits.append((back, [(-1, back - 1)] if back > 9 else []))
        waits.append((k, ([(1, k + 1)] if k < 8 else []) + [(16, 16 + k)]))
        group = [k, back]
        if k >= 2:
            waits.append((15 + k, []))
            group.append(15 + k)
        table.append((waits, group))
    table.append(([(24, [(1, 25)]), (31, [(-1, 30)])], [24, 31, 32]))
    table.append(([(25, [(1, 26)]), (30, [(-1, 29)])], [25, 30]))
    table.append(([(26, [(1, 27)]), (29, [(-1, 28)])], [26, 29]))
    table.append(([(27, []), (28, [])], [27, 28]))
    return table


ROUNDS = rounds()
SLOT = {0: 0}
for _, group in ROUNDS:
    for j in group:
        SLOT[j] = len(SLOT)


def attention(
    q_ref, k_ref, v_ref, i_ref, o_ref,
    kbuf, vbuf, acc, m_ref, l_ref, sacc, sout, sin_a, sin_b, cs, cr, ss, sr,
):
    s, t, x, c, y, z = coords()

    def at(shift):
        return lax.rem(s + shift + NS, NS)

    barrier = pltpu.get_barrier_semaphore()
    for shift in (1, -1, 16, -16, 32):
        pl.semaphore_signal(barrier, inc=1, device_id=(at(shift), t), device_id_type=MESH)
    own = pl.ds(0, TQ)
    kbuf[own] = k_ref[...]
    vbuf[own] = v_ref[...]
    pl.semaphore_wait(barrier, 5)

    def rows(j):
        return pl.ds(SLOT[j] * TQ, TQ)

    def copy(kv, j, shift, there):
        buf = (kbuf, vbuf)[kv]
        return remote(buf.at[rows(j)], buf.at[rows(there)], cs.at[kv, there], cr.at[kv, there], at(shift), t)

    sends = []

    def send(kv, j, shift, there):
        copy(kv, j, shift, there).start()
        if kv == 0:
            sends.append((j, shift, there))

    for kv in range(2):
        send(kv, 0, 1, 1)
        send(kv, 0, 16, 16)
    for kv in range(2):
        send(kv, 0, 32, 32)

    scale = HD ** (-0.5) * LOG2E
    q_row = lax.broadcasted_iota(jnp.int32, (TQ, TQ), 0)
    k_col = lax.broadcasted_iota(jnp.int32, (TQ, TQ), 1)

    def attend(keys, values, count, masks, first=False):
        def body(g, carry):
            r = pl.ds(pl.multiple_of(g * TQ, TQ), TQ)
            scores = nt_dot(q_ref[r], keys[...]) * scale
            tiles = []
            for i in range(count):
                tile = scores[:, i * TQ : (i + 1) * TQ]
                if masks[i] is not None:
                    tile = jnp.where(masks[i](), tile, -1e30)
                tiles.append(tile)
            top = tiles[0]
            for tile in tiles[1:]:
                top = jnp.maximum(top, tile)
            top = jnp.broadcast_to(jnp.max(top, axis=1, keepdims=True), (TQ, TQ))
            if not first:
                old = m_ref[r]
                top = jnp.maximum(old, top)
                factor = jnp.exp2(old - top)
            m_ref[r] = top
            weights = [jnp.exp2(tile - top) for tile in tiles]
            summed = weights[0]
            for w in weights[1:]:
                summed = summed + w
            p = jnp.concatenate([w.astype(BF) for w in weights], axis=1) if count > 1 else weights[0].astype(BF)
            out = jnp.dot(p, values[...], preferred_element_type=F32)
            if first:
                l_ref[r] = summed
                acc[r] = out
            else:
                l_ref[r] = l_ref[r] * factor + summed
                acc[r] = acc[r] * factor + out
            return carry

        lax.fori_loop(0, G, body, 0, unroll=2)

    def mask_of(j):
        if j == 0:
            return lambda: k_col <= q_row
        if j == 32:
            return lambda: k_col > q_row
        return None

    def group_attend(group):
        n = len(group)
        start = SLOT[group[0]]
        span = pl.ds(start * TQ, n * TQ)

        @pl.when(s >= max(group))
        def _():
            attend(kbuf.at[span], vbuf.at[span], n, [mask_of(j) for j in group])

        @pl.when(s < max(group))
        def _():
            for j in group:
                @pl.when(s >= j)
                def _(j=j):
                    attend(kbuf.at[rows(j)], vbuf.at[rows(j)], 1, [mask_of(j)])

    sink_row = i_ref[...]

    def extract(j):
        base = (s - j) * TQ
        for i in range(NSINK // TQ):
            part = jnp.broadcast_to(sink_row[:, i * TQ : (i + 1) * TQ], (TQ, TQ)).astype(F32)
            column = jnp.transpose(part) - base.astype(F32)
            hot = jnp.where(column == k_col.astype(F32), 1.0, 0.0).astype(BF)
            r = pl.ds(i * TQ, TQ)
            for kv in range(2):
                picked = jnp.dot(hot, (kbuf, vbuf)[kv][rows(j)], preferred_element_type=F32)
                if j == 0:
                    sacc[kv, r] = picked
                else:
                    sacc[kv, r] += picked

    attend(kbuf.at[own], vbuf.at[own], 1, [mask_of(0)], first=True)

    @pl.when(y < 2)
    def _():
        extract(0)

    def sink_copy(dst, n, shift):
        return remote(sout, dst, ss.at[n], sr.at[n], at(shift), t)

    for index, (waits, group) in enumerate(ROUNDS):
        for kv in range(2):
            for j, onward in waits:
                copy(kv, j, 1, j).wait_recv()
                for shift, there in onward:
                    send(kv, j, shift, there)
        group_attend(group)
        for j in group:
            if j < 16:
                @pl.when((y < 2) & (s >= j))
                def _(j=j):
                    extract(j)
        if index == 7:
            @pl.when(y < 2)
            def _():
                sout[...] = sacc[...].astype(BF)

            @pl.when(y == 0)
            def _():
                sink_copy(sin_a, 0, 32).start()
                sink_copy(sin_a, 1, 48).start()

            @pl.when(y == 1)
            def _():
                sink_copy(sin_b, 2, 32).start()

    @pl.when(y == 2)
    def _():
        sink_copy(sin_a, 0, 32).wait_recv()

    @pl.when(y == 3)
    def _():
        sink_copy(sin_a, 1, 48).wait_recv()
        sink_copy(sin_b, 2, 32).wait_recv()
        sin_a[...] = sin_a[...] + sin_b[...]

    @pl.when(y >= 2)
    def _():
        def sink_mask(i):
            return lambda: sink_row[:, i * TQ : (i + 1) * TQ] <= q_row + (s * TQ - W)

        attend(sin_a.at[0], sin_a.at[1], NSINK // TQ, [sink_mask(i) for i in range(NSINK // TQ)])

    for g in range(G):
        r = pl.ds(g * TQ, TQ)
        total = jnp.sum(l_ref[r], axis=1, keepdims=True)
        o_ref[:, g * HD : (g + 1) * HD] = (acc[r] / total).astype(BF)

    for kv in range(2):
        for j, shift, there in sends:
            copy(kv, j, shift, there).wait_send()

    @pl.when(y == 0)
    def _():
        sink_copy(sin_a, 0, 32).wait_send()
        sink_copy(sin_a, 1, 48).wait_send()

    @pl.when(y == 1)
    def _():
        sink_copy(sin_b, 2, 32).wait_send()


def local(queries, hidden, key_value_weight, key_value_bias, positions, sink_index):
    vmem = pl.BlockSpec(memory_space=pltpu.VMEM)
    dma = pltpu.SemaphoreType.DMA
    flops = 2 * 512 * 512 * DL
    q_rot, k_own, v_own = pl.pallas_call(
        project,
        out_shape=[
            jax.ShapeDtypeStruct((G * TQ, HD), BF),
            jax.ShapeDtypeStruct((TQ, HD), BF),
            jax.ShapeDtypeStruct((TQ, HD), BF),
        ],
        in_specs=[vmem] * 5,
        out_specs=[vmem] * 3,
        scratch_shapes=[
            pltpu.VMEM((NY, TQ, DL), BF),
            pltpu.VMEM((2, 2 * HD, DL), BF),
            pltpu.VMEM((NY, TQ, 2 * HD), F32),
            pltpu.VMEM((NY, TQ, 2 * HD), F32),
            pltpu.VMEM((NY, TQ, 2 * HD), F32),
            pltpu.VMEM((NX, TQ, 2 * HD), F32),
            pltpu.VMEM((TQ, HD), F32),
            pltpu.VMEM((TQ, HD), F32),
            dma((NY,)),
            dma((NY,)),
            dma((9, 2)),
            dma((9, 2)),
            dma((9, 2)),
            dma((9, 2)),
            dma((NY,)),
            dma((NY,)),
            dma((NX,)),
            dma((NX,)),
        ],
        compiler_params=pltpu.CompilerParams(
            collective_id=0, has_side_effects=True, vmem_limit_bytes=32 * 2**20
        ),
        cost_estimate=pl.CostEstimate(flops=flops, bytes_accessed=2**20, transcendentals=2**15),
        name="project",
    )(queries, hidden, jnp.swapaxes(key_value_weight, 1, 2), key_value_bias, positions)
    keys = W + TQ + NSINK
    return pl.pallas_call(
        attention,
        out_shape=jax.ShapeDtypeStruct((TQ, G * HD), BF),
        in_specs=[vmem] * 4,
        out_specs=vmem,
        scratch_shapes=[
            pltpu.VMEM((33 * TQ, HD), BF),
            pltpu.VMEM((33 * TQ, HD), BF),
            pltpu.VMEM((G * TQ, HD), F32),
            pltpu.VMEM((G * TQ, HD), F32),
            pltpu.VMEM((G * TQ, HD), F32),
            pltpu.VMEM((2, NSINK, HD), F32),
            pltpu.VMEM((2, NSINK, HD), BF),
            pltpu.VMEM((2, NSINK, HD), BF),
            pltpu.VMEM((2, NSINK, HD), BF),
            dma((2, 33)),
            dma((2, 33)),
            dma((3,)),
            dma((3,)),
        ],
        compiler_params=pltpu.CompilerParams(
            collective_id=1, has_side_effects=True, vmem_limit_bytes=32 * 2**20
        ),
        cost_estimate=pl.CostEstimate(
            flops=4 * G * TQ * keys * HD, bytes_accessed=2**20, transcendentals=G * TQ * keys
        ),
        name="attention",
    )(q_rot, k_own, v_own, sink_index.reshape(1, NSINK))


def solution(mesh):
    placed = (
        P("seq", "tensor"),
        P("seq", "tensor"),
        P(None, "tensor", "seq"),
        P(None, "tensor"),
        P(None, "seq"),
        P(),
    )
    return jax.shard_map(
        local, mesh=mesh, in_specs=placed, out_specs=P("seq", "tensor"), check_vma=False
    )
```

```python
import functools
import math

import jax
import jax.numpy as jnp
from jax import lax
from jax.experimental import pallas as pl
from jax.experimental.pallas import tpu as pltpu
from jax.sharding import PartitionSpec as P

H = 64
KVH = 8
HD = 128
W = 4096
NX = 4
NY = 4
NZ = 16
NS = NY * NZ
TQ = 128
G = H // KVH
DL = 1024
NSINK = 512
MESH = pl.DeviceIdType.MESH
LOG2E = 1.4426950408889634
BF = jnp.bfloat16
F32 = jnp.float32


def coords():
    s = lax.axis_index("seq")
    t = lax.axis_index("tensor")
    return s, t, t // 2, t % 2, s // NZ, s % NZ


def remote(src, dst, send, recv, seq, tensor):
    return pltpu.make_async_remote_copy(
        src_ref=src,
        dst_ref=dst,
        send_sem=send,
        recv_sem=recv,
        device_id=(seq, tensor),
        device_id_type=MESH,
    )


def nt_dot(a, b):
    return lax.dot_general(a, b, (((1,), (1,)), ((), ())), preferred_element_type=F32)


def rope_tables(pos):
    half = HD // 2
    pair = lax.broadcasted_iota(jnp.int32, (half, TQ), 0)
    inverse = jnp.exp(pair.astype(F32) * (-2.0 * math.log(1000000.0) / HD))
    first = HD // 8
    second = first + 3 * HD // 16
    temporal, height, width = (jnp.broadcast_to(pos[i : i + 1], (half, TQ)) for i in range(3))
    chosen = jnp.where(pair < first, temporal, jnp.where(pair < second, height, width))
    angles = chosen * inverse
    return jnp.cos(angles), jnp.sin(angles)


def rotate(u, tables):
    cosine, sine = tables
    top, low = u[: HD // 2], u[HD // 2 :]
    return jnp.concatenate([top * cosine - low * sine, low * cosine + top * sine], axis=0)


W_ONWARD = {
    0: [1, -1, 2, -2],
    1: [2], 2: [2], 3: [2], 4: [2], 5: [2], 6: [2],
    15: [-2], 14: [-2], 13: [-2], 12: [-2], 11: [-2],
}
W_ROUNDS = [[1, 15, 2, 14], [3, 13, 4, 12], [5, 11, 6, 10], [7, 9, 8]]


def project(
    q_ref, h_ref, w_ref, b_ref, p_ref, qo_ref, kv_ref,
    hid, wbuf, p3s, p3r, p4s, p4r, pos, bias, kvs, kvr,
    hs, hr, ws, wr, p3ss, p3rs, p4ss, p4rs, ps, pr, ts, tr,
):
    s, t, x, c, y, z = coords()
    other = x * 2 + (1 - c)
    mine = x == y

    def on_z(d):
        return y * NZ + lax.rem(z + d + NZ, NZ)

    def on_y(d):
        return lax.rem(y + d, NY) * NZ + z

    def on_x(d):
        return lax.rem(x + d, NX) * 2 + c

    barrier = pltpu.get_barrier_semaphore()

    def greet(seq, tensor):
        pl.semaphore_signal(barrier, inc=1, device_id=(seq, tensor), device_id_type=MESH)

    greet(s, other)
    for d in (1, -1, 2, -2):
        greet(on_z(d), t)
    for d in range(1, NY):
        greet(on_y(d), t)
        greet(s, on_x(d))

    @pl.when(jnp.logical_not(mine))
    def _():
        greet(x * NZ + z, y * 2 + c)

    wbuf[z // 8, lax.rem(z, 8)] = w_ref[...]
    hid[y] = h_ref[...]
    pos[0:3] = p_ref[...].astype(F32)
    pos[3:8] = jnp.zeros((5, TQ), F32)
    own_tables = rope_tables(pos[0:8])
    bias[0:2] = b_ref[...].astype(F32)
    bias[2:8] = jnp.zeros((6, HD), F32)
    pl.semaphore_wait(barrier, jnp.where(mine, 11, 12))

    def w_block(d):
        origin = lax.rem(z - d + NZ, NZ)
        return wbuf.at[origin // 8, lax.rem(origin, 8)]

    def w_copy(kv, d, hop):
        there = (d + hop) % NZ
        block = w_block(d).at[kv]
        return remote(block, block, ws.at[kv, there], wr.at[kv, there], on_z(hop), t)

    def w_forward(kv, d):
        for hop in W_ONWARD.get(d, []):
            w_copy(kv, d, hop).start()

    def w_wait(kv, d):
        block = w_block(d).at[kv]
        remote(block, block, ws.at[kv, d], wr.at[kv, d], s, t).wait_recv()

    for kv in range(2):
        w_forward(kv, 0)

    def h_copy(d):
        return remote(h_ref, hid.at[y], hs.at[d], hr.at[d], on_y(d), t)

    for d in (1, 3, 2):
        h_copy(d).start()

    def p_copy(d):
        return remote(pos.at[pl.ds(0, 8)], pos.at[pl.ds(8, 8)], ps.at[0, d], pr.at[0], on_y(d), t)

    def b_copy(d):
        return remote(bias.at[pl.ds(0, 8)], bias.at[pl.ds(8, 8)], ps.at[1, d], pr.at[1], s, on_x(d))

    @pl.when(mine)
    def _():
        pos[8:16] = pos[0:8]
        bias[8:16] = bias[0:8]
        for d in range(1, NY):
            p_copy(d).start()
            b_copy(d).start()

    def turn_query(g):
        u = jnp.transpose(q_ref[:, g * HD : (g + 1) * HD].astype(F32))
        qo_ref[:, g * TQ : (g + 1) * TQ] = rotate(u, own_tables).astype(BF)

    for index, arrived in enumerate(W_ROUNDS):
        for kv in range(2):
            for d in arrived:
                w_wait(kv, d)
                w_forward(kv, d)
        share = -(-G // (len(W_ROUNDS) - 1))
        for g in range(index * share, min((index + 1) * share, G)):
            turn_query(g)

    @pl.when(jnp.logical_not(mine))
    def _():
        p_copy(1).wait_recv()
        b_copy(1).wait_recv()

    tables = rope_tables(pos[8:16])
    for d in range(1, NY):
        slot = hid.at[lax.rem(y + NY - d, NY)]
        remote(slot, slot, hs.at[d], hr.at[d], s, t).wait_recv()

    def product(head, out):
        rows = hid[...].reshape(NY * TQ, DL)
        for kv in range(2):
            cols = wbuf[head, :, kv].reshape(HD, DL)
            part = nt_dot(rows, cols).reshape(NY, TQ, HD)
            for i in range(NY):
                out[i, kv] = part[i]

    def p3_copy(i):
        return remote(p3s.at[i], p3r.at[i], p3ss.at[i], p3rs.at[i], s, other)

    product(1 - c, p3s)
    for i in range(NY):
        p3_copy(i).start()
    product(c, p4s)

    def p4_copy(i):
        return remote(p4s.at[i], p4r.at[x], p4ss.at[i], p4rs.at[x], s, i * 2 + c)

    for i in range(NY):
        p3_copy(i).wait_recv()
        p4s[i] += p3r[i]

        @pl.when(x == i)
        def _(i=i):
            p4r[x] = p4s[i]

        @pl.when(x != i)
        def _(i=i):
            p4_copy(i).start()

    for i in range(NX):
        @pl.when(x != i)
        def _(i=i):
            remote(p4r.at[i], p4r.at[i], p4ss.at[i], p4rs.at[i], s, t).wait_recv()

    keys = (p4r[0, 0] + p4r[1, 0]) + (p4r[2, 0] + p4r[3, 0]) + bias[8:9]
    kvs[0] = jnp.transpose(rotate(jnp.transpose(keys), tables)).astype(BF)
    vals = (p4r[0, 1] + p4r[1, 1]) + (p4r[2, 1] + p4r[3, 1]) + bias[9:10]
    kvs[1] = jnp.transpose(vals).astype(BF)

    def t_copy():
        return remote(kvs, kvr, ts, tr, x * NZ + z, y * 2 + c)

    @pl.when(mine)
    def _():
        kv_ref[...] = kvs[...]

    @pl.when(jnp.logical_not(mine))
    def _():
        t_copy().start()
        t_copy().wait_recv()
        kv_ref[...] = kvr[...]

    for d, hops in W_ONWARD.items():
        for hop in hops:
            for kv in range(2):
                w_copy(kv, d, hop).wait_send()
    for d in range(1, NY):
        h_copy(d).wait_send()
    for i in range(NY):
        p3_copy(i).wait_send()

        @pl.when(x != i)
        def _(i=i):
            p4_copy(i).wait_send()

    @pl.when(mine)
    def _():
        for d in range(1, NY):
            p_copy(d).wait_send()
            b_copy(d).wait_send()

    @pl.when(jnp.logical_not(mine))
    def _():
        t_copy().wait_send()


ONWARD = {
    0: [(1, 1), (16, 16), (32, 32)],
    16: [(-1, 15)],
    32: [(-1, 31)],
    1: [(1, 2), (16, 17)],
    2: [(1, 3), (16, 18)],
    3: [(1, 4), (16, 19)],
    4: [(1, 5), (16, 20)],
    5: [(1, 6), (16, 21)],
    6: [(1, 7), (16, 22)],
    7: [(1, 8), (16, 23)],
    8: [(16, 24)],
    15: [(-1, 14)],
    14: [(-1, 13)],
    13: [(-1, 12)],
    12: [(-1, 11)],
    11: [(-1, 10)],
    10: [(-1, 9)],
    31: [(-1, 30)],
    30: [(-1, 29)],
    29: [(-1, 28)],
    28: [(-1, 27)],
    27: [(-1, 26)],
    26: [(-1, 25)],
}
ROUNDS = [
    ([1, 16], [1, 16]),
    ([2, 15, 32], [2, 15]),
    ([3, 14, 31], [3, 14]),
    ([17], [17, 31]),
    ([4, 13, 30], [4, 13]),
    ([18], [18, 30]),
    ([5, 12, 29], [5, 12]),
    ([19], [19, 29]),
    ([6, 11, 28], [6, 11]),
    ([20], [20, 28]),
    ([7, 10, 27], [7, 10]),
    ([21], [21, 27]),
    ([8, 9, 26], [8, 9]),
    ([22], [22, 26]),
    ([25, 23, 24], [23, 24, 25, 32]),
]
SINKS_AFTER = 12
SLOT = {0: 0}
for _, group in ROUNDS:
    for j in group:
        SLOT[j] = len(SLOT)


def attention(
    q_ref, kv_ref, i_ref, o_ref,
    buf, acc, m_ref, l_ref, column, sacc_k, sacc_v, out_k, out_v, in_k, in_v, more_k, more_v, cs, cr, ss, sr,
):
    s, t, x, c, y, z = coords()

    def at(shift):
        return lax.rem(s + shift + NS, NS)

    barrier = pltpu.get_barrier_semaphore()
    for shift in (1, -1, 2, -2, 16, -16, 32):
        pl.semaphore_signal(barrier, inc=1, device_id=(at(shift), t), device_id_type=MESH)
    buf[0] = kv_ref[...]
    pl.semaphore_wait(barrier, 7)

    def copy(kv, j, shift, there):
        src, dst = buf.at[SLOT[j], kv], buf.at[SLOT[there], kv]
        return remote(src, dst, cs.at[kv, there], cr.at[kv, there], at(shift), t)

    def forward(kv, j):
        for shift, there in ONWARD.get(j, []):
            copy(kv, j, shift, there).start()

    for kv in range(2):
        forward(kv, 0)

    sink_row = i_ref[...]
    for i in range(NSINK // TQ):
        part = jnp.broadcast_to(sink_row[:, i * TQ : (i + 1) * TQ], (TQ, TQ)).astype(F32)
        column[i] = jnp.transpose(part)

    scale = HD ** (-0.5)
    k_row = lax.broadcasted_iota(jnp.int32, (TQ, TQ), 0)
    q_col = lax.broadcasted_iota(jnp.int32, (TQ, TQ), 1)

    def attend(keys, values, masks, first=False):
        n = len(masks)
        for g in range(G):
            cols = slice(g * TQ, (g + 1) * TQ)
            scores = jnp.dot(keys(), q_ref[:, cols], preferred_element_type=F32)
            tiles = []
            for i, mask in enumerate(masks):
                tile = scores[i * TQ : (i + 1) * TQ]
                tiles.append(tile if mask is None else jnp.where(mask(), tile, -1e30))
            scores = jnp.concatenate(tiles, axis=0).reshape(n * TQ // 8, 8, TQ)
            top = jnp.max(jnp.max(scores, axis=0), axis=0, keepdims=True) * scale
            top = jnp.broadcast_to(top, (8, TQ))
            if not first:
                old = m_ref[:, cols]
                top = jnp.maximum(old, top)
                factor = jnp.exp(old - top)
            m_ref[:, cols] = top
            weights = jnp.exp(scores * scale - top[None])
            summed = jnp.sum(weights, axis=0)
            out = jnp.dot(values(), weights.reshape(n * TQ, TQ).astype(BF), preferred_element_type=F32)
            if first:
                l_ref[:, cols] = summed
                acc[:, cols] = out
            else:
                l_ref[:, cols] = l_ref[:, cols] * factor + summed
                scaled = acc[:, cols].reshape(HD // 8, 8, TQ) * factor[None]
                acc[:, cols] = scaled.reshape(HD, TQ) + out

    def attend_blocks(group, masks, first=False):
        start, n = SLOT[group[0]], len(group)
        attend(
            lambda: buf[start : start + n, 0].reshape(n * TQ, HD),
            lambda: jnp.concatenate([buf[start + i, 1] for i in range(n)], axis=1),
            masks,
            first,
        )

    def mask_of(j, guard):
        if j == 32:
            return lambda: (k_row > q_col) & (s >= 32)
        return (lambda: jnp.broadcast_to(s >= j, (TQ, TQ))) if guard else None

    def group_attend(group):
        @pl.when(s >= max(group))
        def _():
            attend_blocks(group, [mask_of(j, False) for j in group])

        @pl.when((s >= min(group)) & (s < max(group)))
        def _():
            attend_blocks(group, [mask_of(j, True) for j in group])

    def extract(j):
        base = (s - j) * TQ
        token = (q_col + base).astype(F32)
        hot = jnp.concatenate(
            [jnp.where(column[i] == token, 1.0, 0.0).astype(BF) for i in range(NSINK // TQ)], axis=0
        )
        k_part = jnp.dot(hot, buf[SLOT[j], 0], preferred_element_type=F32)
        across = jnp.broadcast_to(sink_row, (TQ, NSINK)) - base
        hot = jnp.where(across == lax.broadcasted_iota(jnp.int32, (TQ, NSINK), 0), 1.0, 0.0).astype(BF)
        v_part = jnp.dot(buf[SLOT[j], 1], hot, preferred_element_type=F32)
        if j == 0:
            sacc_k[...] = k_part
            sacc_v[...] = v_part
        else:
            sacc_k[...] += k_part
            sacc_v[...] += v_part

    attend_blocks([0], [lambda: k_row <= q_col], first=True)

    @pl.when(y < 2)
    def _():
        extract(0)

    def sink_copies(more, n, shift):
        dst_k, dst_v = (more_k, more_v) if more else (in_k, in_v)
        return (
            remote(out_k, dst_k, ss.at[n, 0], sr.at[n, 0], at(shift), t),
            remote(out_v, dst_v, ss.at[n, 1], sr.at[n, 1], at(shift), t),
        )

    for index, (waits, group) in enumerate(ROUNDS):
        for kv in range(2):
            for j in waits:
                copy(kv, j, 1, j).wait_recv()
                forward(kv, j)
        group_attend(group)
        for j in group:
            if j < 16:
                @pl.when((y < 2) & (s >= j))
                def _(j=j):
                    extract(j)
        if index == SINKS_AFTER:
            @pl.when(y < 2)
            def _():
                out_k[...] = sacc_k[...].astype(BF)
                out_v[...] = sacc_v[...].astype(BF)

            @pl.when(y == 0)
            def _():
                for one in sink_copies(False, 1, 48) + sink_copies(False, 0, 32):
                    one.start()

            @pl.when(y == 1)
            def _():
                for one in sink_copies(True, 2, 32):
                    one.start()

    @pl.when(y == 2)
    def _():
        for one in sink_copies(False, 0, 32):
            one.wait_recv()

    @pl.when(y == 3)
    def _():
        for one in sink_copies(False, 1, 48) + sink_copies(True, 2, 32):
            one.wait_recv()
        in_k[...] = in_k[...] + more_k[...]
        in_v[...] = in_v[...] + more_v[...]

    @pl.when(y >= 2)
    def _():
        limit = (q_col + (s * TQ - W)).astype(F32)
        attend(
            lambda: in_k[...],
            lambda: in_v[...],
            [lambda i=i: column[i] <= limit for i in range(NSINK // TQ)],
        )

    for g in range(G):
        cols = slice(g * TQ, (g + 1) * TQ)
        total = jnp.sum(l_ref[:, cols], axis=0, keepdims=True)
        o_ref[:, cols] = jnp.transpose(acc[:, cols] / total).astype(BF)

    for j, moves in ONWARD.items():
        for shift, there in moves:
            for kv in range(2):
                copy(kv, j, shift, there).wait_send()

    @pl.when(y == 0)
    def _():
        for one in sink_copies(False, 1, 48) + sink_copies(False, 0, 32):
            one.wait_send()

    @pl.when(y == 1)
    def _():
        for one in sink_copies(True, 2, 32):
            one.wait_send()


def local(queries, hidden, key_value_weight, key_value_bias, positions, sink_index):
    vmem = pl.BlockSpec(memory_space=pltpu.VMEM)
    dma = pltpu.SemaphoreType.DMA
    flops = 2 * 512 * 512 * DL
    q_turned, own = pl.pallas_call(
        project,
        out_shape=[
            jax.ShapeDtypeStruct((HD, G * TQ), BF),
            jax.ShapeDtypeStruct((2, TQ, HD), BF),
        ],
        in_specs=[vmem] * 5,
        out_specs=[vmem] * 2,
        scratch_shapes=[
            pltpu.VMEM((NY, TQ, DL), BF),
            pltpu.VMEM((2, 8, 2, 16, DL), BF),
            pltpu.VMEM((NY, 2, TQ, HD), F32),
            pltpu.VMEM((NY, 2, TQ, HD), F32),
            pltpu.VMEM((NY, 2, TQ, HD), F32),
            pltpu.VMEM((NX, 2, TQ, HD), F32),
            pltpu.VMEM((16, TQ), F32),
            pltpu.VMEM((16, HD), F32),
            pltpu.VMEM((2, TQ, HD), BF),
            pltpu.VMEM((2, TQ, HD), BF),
            dma((NY,)),
            dma((NY,)),
            dma((2, NZ)),
            dma((2, NZ)),
            dma((NY,)),
            dma((NY,)),
            dma((NX,)),
            dma((NX,)),
            dma((2, NY)),
            dma((2,)),
            dma,
            dma,
        ],
        compiler_params=pltpu.CompilerParams(
            collective_id=0, has_side_effects=True, vmem_limit_bytes=32 * 2**20
        ),
        cost_estimate=pl.CostEstimate(flops=flops, bytes_accessed=2**20, transcendentals=2**15),
        name="project",
    )(queries, hidden, jnp.swapaxes(key_value_weight, 1, 2), key_value_bias, positions)
    keys = W + TQ + NSINK
    return pl.pallas_call(
        attention,
        out_shape=jax.ShapeDtypeStruct((TQ, G * HD), BF),
        in_specs=[vmem] * 3,
        out_specs=vmem,
        scratch_shapes=[
            pltpu.VMEM((33, 2, TQ, HD), BF),
            pltpu.VMEM((HD, G * TQ), F32),
            pltpu.VMEM((8, G * TQ), F32),
            pltpu.VMEM((8, G * TQ), F32),
            pltpu.VMEM((NSINK // TQ, TQ, TQ), F32),
            pltpu.VMEM((NSINK, HD), F32),
            pltpu.VMEM((HD, NSINK), F32),
        ]
        + [pltpu.VMEM((NSINK, HD), BF), pltpu.VMEM((HD, NSINK), BF)] * 3
        + [dma((2, 33)), dma((2, 33)), dma((3, 2)), dma((3, 2))],
        compiler_params=pltpu.CompilerParams(
            collective_id=1, has_side_effects=True, vmem_limit_bytes=32 * 2**20
        ),
        cost_estimate=pl.CostEstimate(
            flops=4 * G * TQ * keys * HD, bytes_accessed=2**20, transcendentals=G * TQ * keys
        ),
        name="attention",
    )(q_turned, own, sink_index.reshape(1, NSINK))


def solution(mesh):
    placed = (
        P("seq", "tensor"),
        P("seq", "tensor"),
        P(None, "tensor", "seq"),
        P(None, "tensor"),
        P(None, "seq"),
        P(),
    )
    return jax.shard_map(
        local, mesh=mesh, in_specs=placed, out_specs=P("seq", "tensor"), check_vma=False
    )
```

```python
import functools
import math

import jax
import jax.numpy as jnp
from jax import lax
from jax.experimental import pallas as pl
from jax.experimental.pallas import tpu as pltpu
from jax.sharding import PartitionSpec as P

H = 64
KVH = 8
HD = 128
W = 4096
NX = 4
NY = 4
NZ = 16
NS = NY * NZ
TQ = 128
G = H // KVH
DL = 1024
NSINK = 512
MESH = pl.DeviceIdType.MESH
LOG2E = 1.4426950408889634
BF = jnp.bfloat16
F32 = jnp.float32


def coords():
    s = lax.axis_index("seq")
    t = lax.axis_index("tensor")
    return s, t, t // 2, t % 2, s // NZ, s % NZ


def remote(src, dst, send, recv, seq, tensor):
    return pltpu.make_async_remote_copy(
        src_ref=src,
        dst_ref=dst,
        send_sem=send,
        recv_sem=recv,
        device_id=(seq, tensor),
        device_id_type=MESH,
    )


def nt_dot(a, b):
    return lax.dot_general(a, b, (((1,), (1,)), ((), ())), preferred_element_type=F32)


def rope_tables(pos):
    half = HD // 2
    pair = lax.broadcasted_iota(jnp.int32, (half, TQ), 0)
    inverse = jnp.exp(pair.astype(F32) * (-2.0 * math.log(1000000.0) / HD))
    first = HD // 8
    second = first + 3 * HD // 16
    temporal, height, width = (jnp.broadcast_to(pos[i : i + 1], (half, TQ)) for i in range(3))
    chosen = jnp.where(pair < first, temporal, jnp.where(pair < second, height, width))
    angles = chosen * inverse
    return jnp.cos(angles), jnp.sin(angles)


def rotate(u, tables):
    cosine, sine = tables
    top, low = u[: HD // 2], u[HD // 2 :]
    return jnp.concatenate([top * cosine - low * sine, low * cosine + top * sine], axis=0)


W_ONWARD = {
    0: [1, -1, 2, -2],
    1: [2], 2: [2], 3: [2], 4: [2], 5: [2], 6: [2],
    15: [-2], 14: [-2], 13: [-2], 12: [-2], 11: [-2],
}
W_ROUNDS = [[1, 15, 2, 14], [3, 13, 4, 12], [5, 11, 6, 10], [7, 9, 8]]


def project(
    q_hbm, h_hbm, w_hbm, b_hbm, p_hbm, i_hbm, qo_ref, first_block, sinks,
    q_ref, b_ref, p_ref, hid, wbuf, p3s, p3r, p4s, p4r, pos, bias, kvs,
    ins, hs, hr, ws, wr, p3ss, p3rs, p4ss, p4rs, ps, pr, ts, tr,
):
    s, t, x, c, y, z = coords()
    other = x * 2 + (1 - c)
    mine = x == y

    def on_z(d):
        return y * NZ + lax.rem(z + d + NZ, NZ)

    def on_y(d):
        return lax.rem(y + d, NY) * NZ + z

    def on_x(d):
        return lax.rem(x + d, NX) * 2 + c

    barrier = pltpu.get_barrier_semaphore()

    def greet(seq, tensor):
        pl.semaphore_signal(barrier, inc=1, device_id=(seq, tensor), device_id_type=MESH)

    own_w = wbuf.at[z // 8, lax.rem(z, 8)]
    loads = [
        pltpu.make_async_copy(src, dst, ins.at[i])
        for i, (src, dst) in enumerate(
            [(w_hbm, own_w), (h_hbm, hid.at[y]), (p_hbm, p_ref), (b_hbm, b_ref), (q_hbm, q_ref), (i_hbm, sinks)]
        )
    ]
    for load in loads:
        load.start()
    greet(s, other)
    for d in (1, -1):
        greet(lax.rem(s + d + NS, NS), t)
    for d in (1, -1, 2, -2):
        greet(on_z(d), t)
    for d in range(1, NY):
        greet(on_y(d), t)
        greet(s, on_x(d))

    @pl.when(jnp.logical_not(mine))
    def _():
        greet(x * NZ + z, y * 2 + c)

    pl.semaphore_wait(barrier, jnp.where(mine, 13, 14))
    loads[0].wait()

    def w_block(d):
        origin = lax.rem(z - d + NZ, NZ)
        return wbuf.at[origin // 8, lax.rem(origin, 8)]

    def w_copy(kv, d, hop):
        there = (d + hop) % NZ
        block = w_block(d).at[kv]
        return remote(block, block, ws.at[kv, there], wr.at[kv, there], on_z(hop), t)

    def w_forward(kv, d):
        for hop in W_ONWARD.get(d, []):
            w_copy(kv, d, hop).start()

    def w_wait(kv, d):
        block = w_block(d).at[kv]
        remote(block, block, ws.at[kv, d], wr.at[kv, d], s, t).wait_recv()

    for kv in range(2):
        w_forward(kv, 0)

    def h_copy(d):
        return remote(hid.at[y], hid.at[y], hs.at[d], hr.at[d], on_y(d), t)

    loads[1].wait()
    for d in (1, 3, 2):
        h_copy(d).start()
    for load in loads[2:]:
        load.wait()
    pos[0:3] = p_ref[...].astype(F32)
    pos[3:8] = jnp.zeros((5, TQ), F32)
    bias[0:2] = b_ref[...].astype(F32)
    bias[2:8] = jnp.zeros((6, HD), F32)

    def p_copy(d):
        return remote(pos.at[pl.ds(0, 8)], pos.at[pl.ds(8, 8)], ps.at[0, d], pr.at[0], on_y(d), t)

    def b_copy(d):
        return remote(bias.at[pl.ds(0, 8)], bias.at[pl.ds(8, 8)], ps.at[1, d], pr.at[1], s, on_x(d))

    @pl.when(mine)
    def _():
        pos[8:16] = pos[0:8]
        bias[8:16] = bias[0:8]
        for d in range(1, NY):
            p_copy(d).start()
            b_copy(d).start()

    own_tables = rope_tables(pos[0:8])

    def turn_query(g):
        u = jnp.transpose(q_ref[:, g * HD : (g + 1) * HD].astype(F32))
        qo_ref[:, g * TQ : (g + 1) * TQ] = rotate(u, own_tables).astype(BF)

    for index, arrived in enumerate(W_ROUNDS):
        for kv in range(2):
            for d in arrived:
                w_wait(kv, d)
                w_forward(kv, d)
        share = -(-G // (len(W_ROUNDS) - 1))
        for g in range(index * share, min((index + 1) * share, G)):
            turn_query(g)

    @pl.when(jnp.logical_not(mine))
    def _():
        p_copy(1).wait_recv()
        b_copy(1).wait_recv()

    tables = rope_tables(pos[8:16])
    for d in range(1, NY):
        slot = hid.at[lax.rem(y + NY - d, NY)]
        remote(slot, slot, hs.at[d], hr.at[d], s, t).wait_recv()

    def product(head, out):
        rows = hid[...].reshape(NY * TQ, DL)
        for kv in range(2):
            cols = wbuf[head, :, kv].reshape(HD, DL)
            part = nt_dot(rows, cols).reshape(NY, TQ, HD)
            for i in range(NY):
                out[i, kv] = part[i]

    def p3_copy(i):
        return remote(p3s.at[i], p3r.at[i], p3ss.at[i], p3rs.at[i], s, other)

    product(1 - c, p3s)
    for i in range(NY):
        p3_copy(i).start()
    product(c, p4s)

    def p4_copy(i):
        return remote(p4s.at[i], p4r.at[x], p4ss.at[i], p4rs.at[x], s, i * 2 + c)

    for i in range(NY):
        p3_copy(i).wait_recv()
        p4s[i] += p3r[i]

        @pl.when(x == i)
        def _(i=i):
            p4r[x] = p4s[i]

        @pl.when(x != i)
        def _(i=i):
            p4_copy(i).start()

    for i in range(NX):
        @pl.when(x != i)
        def _(i=i):
            remote(p4r.at[i], p4r.at[i], p4ss.at[i], p4rs.at[i], s, t).wait_recv()

    keys = (p4r[0, 0] + p4r[1, 0]) + (p4r[2, 0] + p4r[3, 0]) + bias[8:9]
    kvs[0] = jnp.transpose(rotate(jnp.transpose(keys), tables)).astype(BF)
    vals = (p4r[0, 1] + p4r[1, 1]) + (p4r[2, 1] + p4r[3, 1]) + bias[9:10]
    kvs[1] = jnp.transpose(vals).astype(BF)

    def t_copy():
        return remote(kvs, first_block, ts, tr, x * NZ + z, y * 2 + c)

    @pl.when(mine)
    def _():
        first_block[...] = kvs[...]

    @pl.when(jnp.logical_not(mine))
    def _():
        t_copy().start()
        t_copy().wait_recv()

    def finish():
        for d, hops in W_ONWARD.items():
            for hop in hops:
                for kv in range(2):
                    w_copy(kv, d, hop).wait_send()
        for d in range(1, NY):
            h_copy(d).wait_send()
        for i in range(NY):
            p3_copy(i).wait_send()

            @pl.when(x != i)
            def _(i=i):
                p4_copy(i).wait_send()

        @pl.when(mine)
        def _():
            for d in range(1, NY):
                p_copy(d).wait_send()
                b_copy(d).wait_send()

        @pl.when(jnp.logical_not(mine))
        def _():
            t_copy().wait_send()

    return finish


ONWARD = {
    0: [(1, 1), (16, 16), (32, 32)],
    16: [(-1, 15)],
    32: [(-1, 31)],
    1: [(1, 2), (16, 17)],
    2: [(1, 3), (16, 18)],
    3: [(1, 4), (16, 19)],
    4: [(1, 5), (16, 20)],
    5: [(1, 6), (16, 21)],
    6: [(1, 7), (16, 22)],
    7: [(1, 8), (16, 23)],
    8: [(16, 24)],
    15: [(-1, 14)],
    14: [(-1, 13)],
    13: [(-1, 12)],
    12: [(-1, 11)],
    11: [(-1, 10)],
    10: [(-1, 9)],
    31: [(-1, 30)],
    30: [(-1, 29)],
    29: [(-1, 28)],
    28: [(-1, 27)],
    27: [(-1, 26)],
    26: [(-1, 25)],
}
ROUNDS = [
    ([1, 16], [1, 16]),
    ([2, 15, 32], [2, 15]),
    ([3, 14, 31], [3, 14]),
    ([17], [17, 31]),
    ([4, 13, 30], [4, 13]),
    ([18], [18, 30]),
    ([5, 12, 29], [5, 12]),
    ([19], [19, 29]),
    ([6, 11, 28], [6, 11]),
    ([20], [20, 28]),
    ([7, 10, 27], [7, 10]),
    ([21], [21, 27]),
    ([8, 9, 26], [8, 9]),
    ([22], [22, 26]),
    ([25, 23, 24], [23, 24, 25, 32]),
]
SINKS_AFTER = 12
SLOT = {0: 0}
for _, group in ROUNDS:
    for j in group:
        SLOT[j] = len(SLOT)


def attention(
    q_ref, i_ref, o_ref,
    buf, acc, m_ref, l_ref, column, sacc_k, sacc_v, out_k, out_v, in_k, in_v, more_k, more_v, cs, cr, ss, sr,
):
    s, t, x, c, y, z = coords()

    def at(shift):
        return lax.rem(s + shift + NS, NS)

    def copy(kv, j, shift, there):
        src, dst = buf.at[SLOT[j], kv], buf.at[SLOT[there], kv]
        return remote(src, dst, cs.at[kv, there], cr.at[kv, there], at(shift), t)

    def forward(kv, j):
        for shift, there in ONWARD.get(j, []):
            copy(kv, j, shift, there).start()

    for kv in range(2):
        forward(kv, 0)

    sink_row = i_ref[...]
    for i in range(NSINK // TQ):
        part = jnp.broadcast_to(sink_row[:, i * TQ : (i + 1) * TQ], (TQ, TQ)).astype(F32)
        column[i] = jnp.transpose(part)

    scale = HD ** (-0.5)
    k_row = lax.broadcasted_iota(jnp.int32, (TQ, TQ), 0)
    q_col = lax.broadcasted_iota(jnp.int32, (TQ, TQ), 1)

    def attend(keys, values, masks, first=False):
        n = len(masks)
        for g in range(G):
            cols = slice(g * TQ, (g + 1) * TQ)
            scores = jnp.dot(keys(), q_ref[:, cols], preferred_element_type=F32)
            tiles = []
            for i, mask in enumerate(masks):
                tile = scores[i * TQ : (i + 1) * TQ]
                tiles.append(tile if mask is None else jnp.where(mask(), tile, -1e30))
            scores = jnp.concatenate(tiles, axis=0).reshape(n * TQ // 8, 8, TQ)
            top = jnp.max(jnp.max(scores, axis=0), axis=0, keepdims=True) * scale
            top = jnp.broadcast_to(top, (8, TQ))
            if not first:
                old = m_ref[:, cols]
                top = jnp.maximum(old, top)
                factor = jnp.exp(old - top)
            m_ref[:, cols] = top
            weights = jnp.exp(scores * scale - top[None])
            summed = jnp.sum(weights, axis=0)
            out = jnp.dot(values(), weights.reshape(n * TQ, TQ).astype(BF), preferred_element_type=F32)
            if first:
                l_ref[:, cols] = summed
                acc[:, cols] = out
            else:
                l_ref[:, cols] = l_ref[:, cols] * factor + summed
                scaled = acc[:, cols].reshape(HD // 8, 8, TQ) * factor[None]
                acc[:, cols] = scaled.reshape(HD, TQ) + out

    def attend_blocks(group, masks, first=False):
        start, n = SLOT[group[0]], len(group)
        attend(
            lambda: buf[start : start + n, 0].reshape(n * TQ, HD),
            lambda: jnp.concatenate([buf[start + i, 1] for i in range(n)], axis=1),
            masks,
            first,
        )

    def mask_of(j, guard):
        if j == 32:
            return lambda: (k_row > q_col) & (s >= 32)
        return (lambda: jnp.broadcast_to(s >= j, (TQ, TQ))) if guard else None

    def group_attend(group):
        @pl.when(s >= max(group))
        def _():
            attend_blocks(group, [mask_of(j, False) for j in group])

        @pl.when((s >= min(group)) & (s < max(group)))
        def _():
            attend_blocks(group, [mask_of(j, True) for j in group])

    def extract(j):
        base = (s - j) * TQ
        token = (q_col + base).astype(F32)
        hot = jnp.concatenate(
            [jnp.where(column[i] == token, 1.0, 0.0).astype(BF) for i in range(NSINK // TQ)], axis=0
        )
        k_part = jnp.dot(hot, buf[SLOT[j], 0], preferred_element_type=F32)
        across = jnp.broadcast_to(sink_row, (TQ, NSINK)) - base
        hot = jnp.where(across == lax.broadcasted_iota(jnp.int32, (TQ, NSINK), 0), 1.0, 0.0).astype(BF)
        v_part = jnp.dot(buf[SLOT[j], 1], hot, preferred_element_type=F32)
        if j == 0:
            sacc_k[...] = k_part
            sacc_v[...] = v_part
        else:
            sacc_k[...] += k_part
            sacc_v[...] += v_part

    attend_blocks([0], [lambda: k_row <= q_col], first=True)

    @pl.when(y < 2)
    def _():
        extract(0)

    def sink_copies(more, n, shift):
        dst_k, dst_v = (more_k, more_v) if more else (in_k, in_v)
        return (
            remote(out_k, dst_k, ss.at[n, 0], sr.at[n, 0], at(shift), t),
            remote(out_v, dst_v, ss.at[n, 1], sr.at[n, 1], at(shift), t),
        )

    for index, (waits, group) in enumerate(ROUNDS):
        for kv in range(2):
            for j in waits:
                copy(kv, j, 1, j).wait_recv()
                forward(kv, j)
        group_attend(group)
        for j in group:
            if j < 16:
                @pl.when((y < 2) & (s >= j))
                def _(j=j):
                    extract(j)
        if index == SINKS_AFTER:
            @pl.when(y < 2)
            def _():
                out_k[...] = sacc_k[...].astype(BF)
                out_v[...] = sacc_v[...].astype(BF)

            @pl.when(y == 0)
            def _():
                for one in sink_copies(False, 1, 48) + sink_copies(False, 0, 32):
                    one.start()

            @pl.when(y == 1)
            def _():
                for one in sink_copies(True, 2, 32):
                    one.start()

    @pl.when(y == 2)
    def _():
        for one in sink_copies(False, 0, 32):
            one.wait_recv()

    @pl.when(y == 3)
    def _():
        for one in sink_copies(False, 1, 48) + sink_copies(True, 2, 32):
            one.wait_recv()
        in_k[...] = in_k[...] + more_k[...]
        in_v[...] = in_v[...] + more_v[...]

    @pl.when(y >= 2)
    def _():
        limit = (q_col + (s * TQ - W)).astype(F32)
        attend(
            lambda: in_k[...],
            lambda: in_v[...],
            [lambda i=i: column[i] <= limit for i in range(NSINK // TQ)],
        )

    for g in range(G):
        cols = slice(g * TQ, (g + 1) * TQ)
        total = jnp.sum(l_ref[:, cols], axis=0, keepdims=True)
        o_ref[:, cols] = jnp.transpose(acc[:, cols] / total).astype(BF)

    for j, moves in ONWARD.items():
        for shift, there in moves:
            for kv in range(2):
                copy(kv, j, shift, there).wait_send()

    @pl.when(y == 0)
    def _():
        for one in sink_copies(False, 1, 48) + sink_copies(False, 0, 32):
            one.wait_send()

    @pl.when(y == 1)
    def _():
        for one in sink_copies(True, 2, 32):
            one.wait_send()


def local(queries, hidden, key_value_weight, key_value_bias, positions, sink_index):
    vmem = pl.BlockSpec(memory_space=pltpu.VMEM)
    hbm = pl.BlockSpec(memory_space=pl.ANY)
    dma = pltpu.SemaphoreType.DMA
    keys = W + TQ + NSINK
    shared = [
        pltpu.VMEM((HD, G * TQ), BF),
        pltpu.VMEM((33, 2, TQ, HD), BF),
        pltpu.VMEM((1, NSINK), jnp.int32),
    ]
    projecting = [
        pltpu.VMEM((TQ, G * HD), BF),
        pltpu.VMEM((2, HD), BF),
        pltpu.VMEM((3, TQ), jnp.int32),
        pltpu.VMEM((NY, TQ, DL), BF),
        pltpu.VMEM((2, 8, 2, 16, DL), BF),
        pltpu.VMEM((NY, 2, TQ, HD), F32),
        pltpu.VMEM((NY, 2, TQ, HD), F32),
        pltpu.VMEM((NY, 2, TQ, HD), F32),
        pltpu.VMEM((NX, 2, TQ, HD), F32),
        pltpu.VMEM((16, TQ), F32),
        pltpu.VMEM((16, HD), F32),
        pltpu.VMEM((2, TQ, HD), BF),
        dma((6,)),
        dma((NY,)),
        dma((NY,)),
        dma((2, NZ)),
        dma((2, NZ)),
        dma((NY,)),
        dma((NY,)),
        dma((NX,)),
        dma((NX,)),
        dma((2, NY)),
        dma((2,)),
        dma,
        dma,
    ]
    attending = [
        pltpu.VMEM((HD, G * TQ), F32),
        pltpu.VMEM((8, G * TQ), F32),
        pltpu.VMEM((8, G * TQ), F32),
        pltpu.VMEM((NSINK // TQ, TQ, TQ), F32),
        pltpu.VMEM((NSINK, HD), F32),
        pltpu.VMEM((HD, NSINK), F32),
    ]
    attending += [pltpu.VMEM((NSINK, HD), BF), pltpu.VMEM((HD, NSINK), BF)] * 3
    attending += [dma((2, 33)), dma((2, 33)), dma((3, 2)), dma((3, 2))]

    def whole(*refs):
        inputs, o_ref, refs = refs[:6], refs[6], refs[7:]
        (turned, buf, sinks), refs = refs[:3], refs[3:]
        finish = project(*inputs, turned, buf.at[0], sinks, *refs[: len(projecting)])
        attention(turned, sinks, o_ref, buf, *refs[len(projecting) :])
        finish()

    return pl.pallas_call(
        whole,
        out_shape=jax.ShapeDtypeStruct((TQ, G * HD), BF),
        in_specs=[hbm] * 6,
        out_specs=vmem,
        scratch_shapes=shared + projecting + attending,
        compiler_params=pltpu.CompilerParams(
            collective_id=0, has_side_effects=True, vmem_limit_bytes=56 * 2**20
        ),
        cost_estimate=pl.CostEstimate(
            flops=4 * G * TQ * keys * HD + 2 * 512 * 512 * DL,
            bytes_accessed=2**20,
            transcendentals=G * TQ * keys,
        ),
        name="windowed",
    )(
        queries,
        hidden,
        jnp.swapaxes(key_value_weight, 1, 2),
        key_value_bias,
        positions,
        sink_index.reshape(1, NSINK),
    )


def solution(mesh):
    placed = (
        P("seq", "tensor"),
        P("seq", "tensor"),
        P(None, "tensor", "seq"),
        P(None, "tensor"),
        P(None, "seq"),
        P(),
    )
    return jax.shard_map(
        local, mesh=mesh, in_specs=placed, out_specs=P("seq", "tensor"), check_vma=False
    )
```

```python
import functools
import math

import jax
import jax.numpy as jnp
from jax import lax
from jax.experimental import pallas as pl
from jax.experimental.pallas import tpu as pltpu
from jax.sharding import PartitionSpec as P

H = 64
KVH = 8
HD = 128
W = 4096
NX = 4
NY = 4
NZ = 16
NS = NY * NZ
TQ = 128
G = H // KVH
DL = 1024
NSINK = 512
MESH = pl.DeviceIdType.MESH
LOG2E = 1.4426950408889634
BF = jnp.bfloat16
F32 = jnp.float32


def coords():
    s = lax.axis_index("seq")
    t = lax.axis_index("tensor")
    return s, t, t // 2, t % 2, s // NZ, s % NZ


def remote(src, dst, send, recv, seq, tensor):
    return pltpu.make_async_remote_copy(
        src_ref=src,
        dst_ref=dst,
        send_sem=send,
        recv_sem=recv,
        device_id=(seq, tensor),
        device_id_type=MESH,
    )


def nt_dot(a, b):
    return lax.dot_general(a, b, (((1,), (1,)), ((), ())), preferred_element_type=F32)


def rope_tables(pos):
    half = HD // 2
    pair = lax.broadcasted_iota(jnp.int32, (half, TQ), 0)
    inverse = jnp.exp(pair.astype(F32) * (-2.0 * math.log(1000000.0) / HD))
    first = HD // 8
    second = first + 3 * HD // 16
    temporal, height, width = (jnp.broadcast_to(pos[i : i + 1], (half, TQ)) for i in range(3))
    chosen = jnp.where(pair < first, temporal, jnp.where(pair < second, height, width))
    angles = chosen * inverse
    return jnp.cos(angles), jnp.sin(angles)


def rotate(u, tables):
    cosine, sine = tables
    top, low = u[: HD // 2], u[HD // 2 :]
    return jnp.concatenate([top * cosine - low * sine, low * cosine + top * sine], axis=0)


W_ONWARD = {
    0: [1, -1, 2, -2],
    1: [2], 2: [2], 3: [2], 4: [2], 5: [2], 6: [2],
    15: [-2], 14: [-2], 13: [-2], 12: [-2], 11: [-2],
}
W_ROUNDS = [[1, 15, 2, 14], [3, 13, 4, 12], [5, 11, 6, 10], [7, 9, 8]]


def project(
    forward, q_hbm, h_hbm, w_hbm, b_hbm, p_hbm, i_hbm, qo_ref, first_block, sinks,
    q_ref, b_ref, p_ref, hid, wbuf, p3s, p3r, p4s, p4r, pos, bias, kvs,
    ins, hs, hr, ws, wr, p3ss, p3rs, p4ss, p4rs, ps, pr, ts, tr,
):
    s, t, x, c, y, z = coords()
    other = x * 2 + (1 - c)
    mine = x == y

    def on_z(d):
        return y * NZ + lax.rem(z + d + NZ, NZ)

    def on_y(d):
        return lax.rem(y + d, NY) * NZ + z

    def on_x(d):
        return lax.rem(x + d, NX) * 2 + c

    barrier = pltpu.get_barrier_semaphore()

    def greet(seq, tensor):
        pl.semaphore_signal(barrier, inc=1, device_id=(seq, tensor), device_id_type=MESH)

    own_w = wbuf.at[z // 8, lax.rem(z, 8)]
    loads = [
        pltpu.make_async_copy(src, dst, ins.at[i])
        for i, (src, dst) in enumerate(
            [(w_hbm, own_w), (h_hbm, hid.at[y]), (p_hbm, p_ref), (b_hbm, b_ref), (q_hbm, q_ref), (i_hbm, sinks)]
        )
    ]
    for load in loads:
        load.start()
    greet(s, other)
    for shift in SHIFTS:
        greet(lax.rem(s - shift + NS, NS), t)
    for d in (1, -1, 2, -2):
        greet(on_z(d), t)
    for d in range(1, NY):
        greet(on_y(d), t)
        greet(s, on_x(d))

    @pl.when(jnp.logical_not(mine))
    def _():
        greet(x * NZ + z, y * 2 + c)

    pl.semaphore_wait(barrier, jnp.where(mine, 11, 12) + len(SHIFTS))
    loads[0].wait()

    def w_block(d):
        origin = lax.rem(z - d + NZ, NZ)
        return wbuf.at[origin // 8, lax.rem(origin, 8)]

    def w_copy(kv, d, hop):
        there = (d + hop) % NZ
        block = w_block(d).at[kv]
        return remote(block, block, ws.at[kv, there], wr.at[kv, there], on_z(hop), t)

    def w_forward(kv, d):
        for hop in W_ONWARD.get(d, []):
            w_copy(kv, d, hop).start()

    def w_wait(kv, d):
        block = w_block(d).at[kv]
        remote(block, block, ws.at[kv, d], wr.at[kv, d], s, t).wait_recv()

    for kv in range(2):
        w_forward(kv, 0)

    def h_copy(d):
        return remote(hid.at[y], hid.at[y], hs.at[d], hr.at[d], on_y(d), t)

    loads[1].wait()
    for d in (1, 3, 2):
        h_copy(d).start()
    for load in loads[2:]:
        load.wait()
    pos[0:3] = p_ref[...].astype(F32)
    pos[3:8] = jnp.zeros((5, TQ), F32)
    bias[0:2] = b_ref[...].astype(F32)
    bias[2:8] = jnp.zeros((6, HD), F32)

    def p_copy(d):
        return remote(pos.at[pl.ds(0, 8)], pos.at[pl.ds(8, 8)], ps.at[0, d], pr.at[0], on_y(d), t)

    def b_copy(d):
        return remote(bias.at[pl.ds(0, 8)], bias.at[pl.ds(8, 8)], ps.at[1, d], pr.at[1], s, on_x(d))

    @pl.when(mine)
    def _():
        pos[8:16] = pos[0:8]
        bias[8:16] = bias[0:8]
        for d in range(1, NY):
            p_copy(d).start()
            b_copy(d).start()

    own_tables = rope_tables(pos[0:8])

    def turn_query(g):
        u = jnp.transpose(q_ref[:, g * HD : (g + 1) * HD].astype(F32))
        qo_ref[:, g * TQ : (g + 1) * TQ] = rotate(u, own_tables).astype(BF)

    for index, arrived in enumerate(W_ROUNDS[:-1]):
        for kv in range(2):
            for d in arrived:
                w_wait(kv, d)
                w_forward(kv, d)
        share = -(-G // (len(W_ROUNDS) - 1))
        for g in range(index * share, min((index + 1) * share, G)):
            turn_query(g)

    @pl.when(jnp.logical_not(mine))
    def _():
        p_copy(1).wait_recv()
        b_copy(1).wait_recv()

    tables = rope_tables(pos[8:16])
    for d in range(1, NY):
        slot = hid.at[lax.rem(y + NY - d, NY)]
        remote(slot, slot, hs.at[d], hr.at[d], s, t).wait_recv()

    def product(kv, head, out):
        rows = hid[...].reshape(NY * TQ, DL)
        cols = wbuf[head, :, kv].reshape(HD, DL)
        part = nt_dot(rows, cols).reshape(NY, TQ, HD)
        for i in range(NY):
            out[kv, i] = part[i]

    def p3_copy(kv, i):
        return remote(p3s.at[kv, i], p3r.at[kv, i], p3ss.at[kv, i], p3rs.at[kv, i], s, other)

    def p4_copy(kv, i):
        return remote(p4s.at[kv, i], p4r.at[kv, x], p4ss.at[kv, i], p4rs.at[kv, x], s, i * 2 + c)

    for kv in range(2):
        for d in W_ROUNDS[-1]:
            w_wait(kv, d)
        product(kv, 1 - c, p3s)
        for i in range(NY):
            p3_copy(kv, i).start()
        product(kv, c, p4s)

    for kv in range(2):
        for i in range(NY):
            p3_copy(kv, i).wait_recv()
            p4s[kv, i] += p3r[kv, i]

            @pl.when(x == i)
            def _(kv=kv, i=i):
                p4r[kv, x] = p4s[kv, i]

            @pl.when(x != i)
            def _(kv=kv, i=i):
                p4_copy(kv, i).start()

    def t_copy(kv):
        return remote(kvs.at[kv], first_block.at[kv], ts.at[kv], tr.at[kv], x * NZ + z, y * 2 + c)

    for kv in range(2):
        for i in range(NX):
            @pl.when(x != i)
            def _(kv=kv, i=i):
                slot = p4r.at[kv, i]
                remote(slot, slot, p4ss.at[kv, i], p4rs.at[kv, i], s, t).wait_recv()

        total = (p4r[kv, 0] + p4r[kv, 1]) + (p4r[kv, 2] + p4r[kv, 3]) + bias[8 + kv : 9 + kv]
        total = jnp.transpose(total)
        if kv == 0:
            total = jnp.transpose(rotate(total, tables))
        kvs[kv] = total.astype(BF)

        @pl.when(mine)
        def _(kv=kv):
            first_block[kv] = kvs[kv]

        @pl.when(jnp.logical_not(mine))
        def _(kv=kv):
            t_copy(kv).start()

    for kv in range(2):
        @pl.when(jnp.logical_not(mine))
        def _(kv=kv):
            t_copy(kv).wait_recv()

        forward(kv, 0)

    def finish():
        for d, hops in W_ONWARD.items():
            for hop in hops:
                for kv in range(2):
                    w_copy(kv, d, hop).wait_send()
        for d in range(1, NY):
            h_copy(d).wait_send()
        for kv in range(2):
            for i in range(NY):
                p3_copy(kv, i).wait_send()

                @pl.when(x != i)
                def _(kv=kv, i=i):
                    p4_copy(kv, i).wait_send()

        @pl.when(mine)
        def _():
            for d in range(1, NY):
                p_copy(d).wait_send()
                b_copy(d).wait_send()

        @pl.when(jnp.logical_not(mine))
        def _():
            for kv in range(2):
                t_copy(kv).wait_send()

    return finish


ONWARD = {
    0: [(1, 1), (16, 16), (32, 32)],
    16: [(-1, 15)],
    32: [(-1, 31)],
    1: [(1, 2), (16, 17)],
    2: [(1, 3), (16, 18)],
    3: [(1, 4), (16, 19)],
    4: [(1, 5), (16, 20)],
    5: [(1, 6), (16, 21)],
    6: [(1, 7), (16, 22)],
    7: [(1, 8), (16, 23)],
    8: [(16, 24)],
    15: [(-1, 14)],
    14: [(-1, 13)],
    13: [(-1, 12)],
    12: [(-1, 11)],
    11: [(-1, 10)],
    10: [(-1, 9)],
    31: [(-1, 30)],
    30: [(-1, 29)],
    29: [(-1, 28)],
    28: [(-1, 27)],
    27: [(-1, 26)],
    26: [(-1, 25)],
}
ROUNDS = [
    ([1, 16], [1, 16]),
    ([2, 15, 32], [2, 15]),
    ([3, 14, 31], [3, 14]),
    ([17], [17, 31]),
    ([4, 13, 30], [4, 13]),
    ([18], [18, 30]),
    ([5, 12, 29], [5, 12]),
    ([19], [19, 29]),
    ([6, 11, 28], [6, 11]),
    ([20], [20, 28]),
    ([7, 10, 27], [7, 10]),
    ([21], [21, 27]),
    ([8, 9, 26], [8, 9]),
    ([22], [22, 26]),
    ([25, 23, 24], [23, 24, 25, 32]),
]
SINKS_AFTER = 12
SHIFTS = sorted({shift % NS for moves in ONWARD.values() for shift, _ in moves} | {32, 48})
SLOT = {0: 0}
for _, group in ROUNDS:
    for j in group:
        SLOT[j] = len(SLOT)


def block_copies(buf, cs, cr):
    s, t, x, c, y, z = coords()

    def copy(kv, j, shift, there):
        src, dst = buf.at[SLOT[j], kv], buf.at[SLOT[there], kv]
        return remote(src, dst, cs.at[kv, there], cr.at[kv, there], lax.rem(s + shift + NS, NS), t)

    def forward(kv, j):
        for shift, there in ONWARD.get(j, []):
            copy(kv, j, shift, there).start()

    return copy, forward


def attention(
    copy, forward, q_ref, i_ref, o_ref,
    buf, acc, m_ref, l_ref, column, sacc_k, sacc_v, out_k, out_v, in_k, in_v, more_k, more_v, ss, sr,
):
    s, t, x, c, y, z = coords()

    def at(shift):
        return lax.rem(s + shift + NS, NS)

    sink_row = i_ref[...]
    for i in range(NSINK // TQ):
        part = jnp.broadcast_to(sink_row[:, i * TQ : (i + 1) * TQ], (TQ, TQ)).astype(F32)
        column[i] = jnp.transpose(part)

    scale = HD ** (-0.5)
    k_row = lax.broadcasted_iota(jnp.int32, (TQ, TQ), 0)
    q_col = lax.broadcasted_iota(jnp.int32, (TQ, TQ), 1)

    def attend(keys, values, masks, first=False):
        n = len(masks)
        for g in range(G):
            cols = slice(g * TQ, (g + 1) * TQ)
            scores = jnp.dot(keys(), q_ref[:, cols], preferred_element_type=F32)
            tiles = []
            for i, mask in enumerate(masks):
                tile = scores[i * TQ : (i + 1) * TQ]
                tiles.append(tile if mask is None else jnp.where(mask(), tile, -1e30))
            scores = jnp.concatenate(tiles, axis=0).reshape(n * TQ // 8, 8, TQ)
            top = jnp.max(jnp.max(scores, axis=0), axis=0, keepdims=True) * scale
            top = jnp.broadcast_to(top, (8, TQ))
            if not first:
                old = m_ref[:, cols]
                top = jnp.maximum(old, top)
                factor = jnp.exp(old - top)
            m_ref[:, cols] = top
            weights = jnp.exp(scores * scale - top[None])
            summed = jnp.sum(weights, axis=0)
            out = jnp.dot(values(), weights.reshape(n * TQ, TQ).astype(BF), preferred_element_type=F32)
            if first:
                l_ref[:, cols] = summed
                acc[:, cols] = out
            else:
                l_ref[:, cols] = l_ref[:, cols] * factor + summed
                scaled = acc[:, cols].reshape(HD // 8, 8, TQ) * factor[None]
                acc[:, cols] = scaled.reshape(HD, TQ) + out

    def attend_blocks(group, masks, first=False):
        start, n = SLOT[group[0]], len(group)
        attend(
            lambda: buf[start : start + n, 0].reshape(n * TQ, HD),
            lambda: jnp.concatenate([buf[start + i, 1] for i in range(n)], axis=1),
            masks,
            first,
        )

    def mask_of(j, guard):
        if j == 32:
            return lambda: (k_row > q_col) & (s >= 32)
        return (lambda: jnp.broadcast_to(s >= j, (TQ, TQ))) if guard else None

    def group_attend(group):
        @pl.when(s >= max(group))
        def _():
            attend_blocks(group, [mask_of(j, False) for j in group])

        @pl.when((s >= min(group)) & (s < max(group)))
        def _():
            attend_blocks(group, [mask_of(j, True) for j in group])

    def extract(j):
        base = (s - j) * TQ
        token = (q_col + base).astype(F32)
        hot = jnp.concatenate(
            [jnp.where(column[i] == token, 1.0, 0.0).astype(BF) for i in range(NSINK // TQ)], axis=0
        )
        k_part = jnp.dot(hot, buf[SLOT[j], 0], preferred_element_type=F32)
        across = jnp.broadcast_to(sink_row, (TQ, NSINK)) - base
        hot = jnp.where(across == lax.broadcasted_iota(jnp.int32, (TQ, NSINK), 0), 1.0, 0.0).astype(BF)
        v_part = jnp.dot(buf[SLOT[j], 1], hot, preferred_element_type=F32)
        if j == 0:
            sacc_k[...] = k_part
            sacc_v[...] = v_part
        else:
            sacc_k[...] += k_part
            sacc_v[...] += v_part

    attend_blocks([0], [lambda: k_row <= q_col], first=True)

    @pl.when(y < 2)
    def _():
        extract(0)

    def sink_copies(more, n, shift):
        dst_k, dst_v = (more_k, more_v) if more else (in_k, in_v)
        return (
            remote(out_k, dst_k, ss.at[n, 0], sr.at[n, 0], at(shift), t),
            remote(out_v, dst_v, ss.at[n, 1], sr.at[n, 1], at(shift), t),
        )

    for index, (waits, group) in enumerate(ROUNDS):
        for kv in range(2):
            for j in waits:
                copy(kv, j, 1, j).wait_recv()
                forward(kv, j)
        group_attend(group)
        for j in group:
            if j < 16:
                @pl.when((y < 2) & (s >= j))
                def _(j=j):
                    extract(j)
        if index == SINKS_AFTER:
            @pl.when(y < 2)
            def _():
                out_k[...] = sacc_k[...].astype(BF)
                out_v[...] = sacc_v[...].astype(BF)

            @pl.when(y == 0)
            def _():
                for one in sink_copies(False, 1, 48) + sink_copies(False, 0, 32):
                    one.start()

            @pl.when(y == 1)
            def _():
                for one in sink_copies(True, 2, 32):
                    one.start()

    @pl.when(y == 2)
    def _():
        for one in sink_copies(False, 0, 32):
            one.wait_recv()

    @pl.when(y == 3)
    def _():
        for one in sink_copies(False, 1, 48) + sink_copies(True, 2, 32):
            one.wait_recv()
        in_k[...] = in_k[...] + more_k[...]
        in_v[...] = in_v[...] + more_v[...]

    @pl.when(y >= 2)
    def _():
        limit = (q_col + (s * TQ - W)).astype(F32)
        attend(
            lambda: in_k[...],
            lambda: in_v[...],
            [lambda i=i: column[i] <= limit for i in range(NSINK // TQ)],
        )

    for g in range(G):
        cols = slice(g * TQ, (g + 1) * TQ)
        total = jnp.sum(l_ref[:, cols], axis=0, keepdims=True)
        o_ref[:, cols] = jnp.transpose(acc[:, cols] / total).astype(BF)

    for j, moves in ONWARD.items():
        for shift, there in moves:
            for kv in range(2):
                copy(kv, j, shift, there).wait_send()

    @pl.when(y == 0)
    def _():
        for one in sink_copies(False, 1, 48) + sink_copies(False, 0, 32):
            one.wait_send()

    @pl.when(y == 1)
    def _():
        for one in sink_copies(True, 2, 32):
            one.wait_send()


def local(queries, hidden, key_value_weight, key_value_bias, positions, sink_index):
    vmem = pl.BlockSpec(memory_space=pltpu.VMEM)
    hbm = pl.BlockSpec(memory_space=pl.ANY)
    dma = pltpu.SemaphoreType.DMA
    keys = W + TQ + NSINK
    shared = [
        pltpu.VMEM((HD, G * TQ), BF),
        pltpu.VMEM((33, 2, TQ, HD), BF),
        pltpu.VMEM((1, NSINK), jnp.int32),
        dma((2, 33)),
        dma((2, 33)),
    ]
    projecting = [
        pltpu.VMEM((TQ, G * HD), BF),
        pltpu.VMEM((2, HD), BF),
        pltpu.VMEM((3, TQ), jnp.int32),
        pltpu.VMEM((NY, TQ, DL), BF),
        pltpu.VMEM((2, 8, 2, 16, DL), BF),
        pltpu.VMEM((2, NY, TQ, HD), F32),
        pltpu.VMEM((2, NY, TQ, HD), F32),
        pltpu.VMEM((2, NY, TQ, HD), F32),
        pltpu.VMEM((2, NX, TQ, HD), F32),
        pltpu.VMEM((16, TQ), F32),
        pltpu.VMEM((16, HD), F32),
        pltpu.VMEM((2, TQ, HD), BF),
        dma((6,)),
        dma((NY,)),
        dma((NY,)),
        dma((2, NZ)),
        dma((2, NZ)),
        dma((2, NY)),
        dma((2, NY)),
        dma((2, NX)),
        dma((2, NX)),
        dma((2, NY)),
        dma((2,)),
        dma((2,)),
        dma((2,)),
    ]
    attending = [
        pltpu.VMEM((HD, G * TQ), F32),
        pltpu.VMEM((8, G * TQ), F32),
        pltpu.VMEM((8, G * TQ), F32),
        pltpu.VMEM((NSINK // TQ, TQ, TQ), F32),
        pltpu.VMEM((NSINK, HD), F32),
        pltpu.VMEM((HD, NSINK), F32),
    ]
    attending += [pltpu.VMEM((NSINK, HD), BF), pltpu.VMEM((HD, NSINK), BF)] * 3
    attending += [dma((3, 2)), dma((3, 2))]

    def whole(*refs):
        inputs, o_ref, refs = refs[:6], refs[6], refs[7:]
        (turned, buf, sinks), refs = refs[:3], refs[3:]
        (cs, cr), refs = refs[:2], refs[2:]
        copy, forward = block_copies(buf, cs, cr)
        finish = project(forward, *inputs, turned, buf.at[0], sinks, *refs[: len(projecting)])
        attention(copy, forward, turned, sinks, o_ref, buf, *refs[len(projecting) :])
        finish()

    return pl.pallas_call(
        whole,
        out_shape=jax.ShapeDtypeStruct((TQ, G * HD), BF),
        in_specs=[hbm] * 6,
        out_specs=vmem,
        scratch_shapes=shared + projecting + attending,
        compiler_params=pltpu.CompilerParams(
            collective_id=0, has_side_effects=True, vmem_limit_bytes=56 * 2**20
        ),
        cost_estimate=pl.CostEstimate(
            flops=4 * G * TQ * keys * HD + 2 * 512 * 512 * DL,
            bytes_accessed=2**20,
            transcendentals=G * TQ * keys,
        ),
        name="windowed",
    )(
        queries,
        hidden,
        jnp.swapaxes(key_value_weight, 1, 2),
        key_value_bias,
        positions,
        sink_index.reshape(1, NSINK),
    )


def solution(mesh):
    placed = (
        P("seq", "tensor"),
        P("seq", "tensor"),
        P(None, "tensor", "seq"),
        P(None, "tensor"),
        P(None, "seq"),
        P(),
    )
    return jax.shard_map(
        local, mesh=mesh, in_specs=placed, out_specs=P("seq", "tensor"), check_vma=False
    )
```

```python
import functools
import math

import jax
import jax.numpy as jnp
from jax import lax
from jax.experimental import pallas as pl
from jax.experimental.pallas import tpu as pltpu
from jax.sharding import PartitionSpec as P

H = 64
KVH = 8
HD = 128
W = 4096
NX = 4
NY = 4
NZ = 16
NS = NY * NZ
TQ = 128
G = H // KVH
DL = 1024
NSINK = 512
MESH = pl.DeviceIdType.MESH
LOG2E = 1.4426950408889634
BF = jnp.bfloat16
F32 = jnp.float32


def coords():
    s = lax.axis_index("seq")
    t = lax.axis_index("tensor")
    return s, t, t // 2, t % 2, s // NZ, s % NZ


def remote(src, dst, send, recv, seq, tensor):
    return pltpu.make_async_remote_copy(
        src_ref=src,
        dst_ref=dst,
        send_sem=send,
        recv_sem=recv,
        device_id=(seq, tensor),
        device_id_type=MESH,
    )


def nt_dot(a, b):
    return lax.dot_general(a, b, (((1,), (1,)), ((), ())), preferred_element_type=F32)


def rope_tables(pos):
    half = HD // 2
    pair = lax.broadcasted_iota(jnp.int32, (half, TQ), 0)
    inverse = jnp.exp(pair.astype(F32) * (-2.0 * math.log(1000000.0) / HD))
    first = HD // 8
    second = first + 3 * HD // 16
    temporal, height, width = (jnp.broadcast_to(pos[i : i + 1], (half, TQ)) for i in range(3))
    chosen = jnp.where(pair < first, temporal, jnp.where(pair < second, height, width))
    angles = chosen * inverse
    return jnp.cos(angles), jnp.sin(angles)


def rotate(u, tables):
    cosine, sine = tables
    top, low = u[: HD // 2], u[HD // 2 :]
    return jnp.concatenate([top * cosine - low * sine, low * cosine + top * sine], axis=0)


W_ONWARD = {
    0: [1, -1, 2, -2],
    1: [2], 2: [2], 3: [2], 4: [2], 5: [2], 6: [2],
    15: [-2], 14: [-2], 13: [-2], 12: [-2], 11: [-2],
}
W_ROUNDS = [[1, 15, 2, 14], [3, 13, 4, 12], [5, 11, 6, 10], [7, 9, 8]]


def project(
    forward, q_hbm, h_hbm, w_hbm, b_hbm, p_hbm, i_hbm, qo_ref, first_block, sinks,
    q_ref, b_ref, p_ref, hid, wbuf, p3s, p3r, p4s, p4r, pos, bias, kvs,
    ins, hs, hr, ws, wr, p3ss, p3rs, p4ss, p4rs, ps, pr, ts, tr,
):
    s, t, x, c, y, z = coords()
    other = x * 2 + (1 - c)
    mine = x == y

    def on_z(d):
        return y * NZ + lax.rem(z + d + NZ, NZ)

    def on_y(d):
        return lax.rem(y + d, NY) * NZ + z

    def on_x(d):
        return lax.rem(x + d, NX) * 2 + c

    barrier = pltpu.get_barrier_semaphore()

    def greet(seq, tensor):
        pl.semaphore_signal(barrier, inc=1, device_id=(seq, tensor), device_id_type=MESH)

    own_w = wbuf.at[z // 8, lax.rem(z, 8)]
    loads = [
        pltpu.make_async_copy(src, dst, ins.at[i])
        for i, (src, dst) in enumerate(
            [(w_hbm, own_w), (h_hbm, hid.at[y]), (p_hbm, p_ref), (b_hbm, b_ref), (q_hbm, q_ref), (i_hbm, sinks)]
        )
    ]
    for load in loads:
        load.start()
    greet(s, other)
    for shift in SHIFTS:
        greet(lax.rem(s - shift + NS, NS), t)
    for d in (1, -1, 2, -2):
        greet(on_z(d), t)
    for d in range(1, NY):
        greet(on_y(d), t)
        greet(s, on_x(d))

    @pl.when(jnp.logical_not(mine))
    def _():
        greet(x * NZ + z, y * 2 + c)

    pl.semaphore_wait(barrier, jnp.where(mine, 11, 12) + len(SHIFTS))
    loads[0].wait()

    def w_block(d):
        origin = lax.rem(z - d + NZ, NZ)
        return wbuf.at[origin // 8, lax.rem(origin, 8)]

    def w_copy(kv, d, hop):
        there = (d + hop) % NZ
        block = w_block(d).at[kv]
        return remote(block, block, ws.at[kv, there], wr.at[kv, there], on_z(hop), t)

    def w_forward(kv, d):
        for hop in W_ONWARD.get(d, []):
            w_copy(kv, d, hop).start()

    def w_wait(kv, d):
        block = w_block(d).at[kv]
        remote(block, block, ws.at[kv, d], wr.at[kv, d], s, t).wait_recv()

    for kv in range(2):
        w_forward(kv, 0)

    def h_copy(d):
        return remote(hid.at[y], hid.at[y], hs.at[d], hr.at[d], on_y(d), t)

    loads[1].wait()
    for d in (1, 3, 2):
        h_copy(d).start()
    for load in loads[2:]:
        load.wait()
    pos[0:3] = p_ref[...].astype(F32)
    pos[3:8] = jnp.zeros((5, TQ), F32)
    bias[0:2] = b_ref[...].astype(F32)
    bias[2:8] = jnp.zeros((6, HD), F32)

    def p_copy(d):
        return remote(pos.at[pl.ds(0, 8)], pos.at[pl.ds(8, 8)], ps.at[0, d], pr.at[0], on_y(d), t)

    def b_copy(d):
        return remote(bias.at[pl.ds(0, 8)], bias.at[pl.ds(8, 8)], ps.at[1, d], pr.at[1], s, on_x(d))

    @pl.when(mine)
    def _():
        pos[8:16] = pos[0:8]
        bias[8:16] = bias[0:8]
        for d in range(1, NY):
            p_copy(d).start()
            b_copy(d).start()

    own_tables = rope_tables(pos[0:8])

    def turn_query(g):
        u = jnp.transpose(q_ref[:, g * HD : (g + 1) * HD].astype(F32))
        qo_ref[:, g * TQ : (g + 1) * TQ] = rotate(u, own_tables).astype(BF)

    for index, arrived in enumerate(W_ROUNDS[:-1]):
        for kv in range(2):
            for d in arrived:
                w_wait(kv, d)
                w_forward(kv, d)
        share = -(-G // (len(W_ROUNDS) - 1))
        for g in range(index * share, min((index + 1) * share, G)):
            turn_query(g)

    @pl.when(jnp.logical_not(mine))
    def _():
        p_copy(1).wait_recv()
        b_copy(1).wait_recv()

    tables = rope_tables(pos[8:16])
    for d in range(1, NY):
        slot = hid.at[lax.rem(y + NY - d, NY)]
        remote(slot, slot, hs.at[d], hr.at[d], s, t).wait_recv()

    def product(kv, head, out):
        rows = hid[...].reshape(NY * TQ, DL)
        cols = wbuf[head, :, kv].reshape(HD, DL)
        part = nt_dot(rows, cols).reshape(NY, TQ, HD)
        for i in range(NY):
            out[kv, i] = part[i]

    def p3_copy(kv, i):
        return remote(p3s.at[kv, i], p3r.at[kv, i], p3ss.at[kv, i], p3rs.at[kv, i], s, other)

    def p4_copy(kv, i):
        return remote(p4s.at[kv, i], p4r.at[kv, x], p4ss.at[kv, i], p4rs.at[kv, x], s, i * 2 + c)

    for kv in range(2):
        for d in W_ROUNDS[-1]:
            w_wait(kv, d)
        product(kv, 1 - c, p3s)
        for i in range(NY):
            p3_copy(kv, i).start()
        product(kv, c, p4s)

    for kv in range(2):
        for i in range(NY):
            p3_copy(kv, i).wait_recv()
            p4s[kv, i] += p3r[kv, i]

            @pl.when(x == i)
            def _(kv=kv, i=i):
                p4r[kv, x] = p4s[kv, i]

            @pl.when(x != i)
            def _(kv=kv, i=i):
                p4_copy(kv, i).start()

    def t_copy(kv):
        return remote(kvs.at[kv], first_block.at[kv], ts.at[kv], tr.at[kv], x * NZ + z, y * 2 + c)

    for kv in range(2):
        for i in range(NX):
            @pl.when(x != i)
            def _(kv=kv, i=i):
                slot = p4r.at[kv, i]
                remote(slot, slot, p4ss.at[kv, i], p4rs.at[kv, i], s, t).wait_recv()

        total = (p4r[kv, 0] + p4r[kv, 1]) + (p4r[kv, 2] + p4r[kv, 3]) + bias[8 + kv : 9 + kv]
        total = jnp.transpose(total)
        if kv == 0:
            total = jnp.transpose(rotate(total, tables))
        kvs[kv] = total.astype(BF)

        @pl.when(mine)
        def _(kv=kv):
            first_block[kv] = kvs[kv]

        @pl.when(jnp.logical_not(mine))
        def _(kv=kv):
            t_copy(kv).start()

    for kv in range(2):
        @pl.when(jnp.logical_not(mine))
        def _(kv=kv):
            t_copy(kv).wait_recv()

        forward(kv, 0)

    def finish():
        for d, hops in W_ONWARD.items():
            for hop in hops:
                for kv in range(2):
                    w_copy(kv, d, hop).wait_send()
        for d in range(1, NY):
            h_copy(d).wait_send()
        for kv in range(2):
            for i in range(NY):
                p3_copy(kv, i).wait_send()

                @pl.when(x != i)
                def _(kv=kv, i=i):
                    p4_copy(kv, i).wait_send()

        @pl.when(mine)
        def _():
            for d in range(1, NY):
                p_copy(d).wait_send()
                b_copy(d).wait_send()

        @pl.when(jnp.logical_not(mine))
        def _():
            for kv in range(2):
                t_copy(kv).wait_send()

    return finish


ONWARD = {
    0: [(1, 1), (16, 16), (32, 32)],
    16: [(-1, 15)],
    32: [(-1, 31)],
    1: [(1, 2), (16, 17)],
    2: [(1, 3), (16, 18)],
    3: [(1, 4), (16, 19)],
    4: [(1, 5), (16, 20)],
    5: [(1, 6), (16, 21)],
    6: [(1, 7), (16, 22)],
    7: [(16, 23)],
    15: [(-1, 14)],
    14: [(-1, 13)],
    13: [(-1, 12)],
    12: [(-1, 11)],
    11: [(-1, 10)],
    10: [(-1, 9)],
    9: [(-1, 8)],
    31: [(-1, 30)],
    30: [(-1, 29)],
    29: [(-1, 28)],
    28: [(-1, 27)],
    27: [(-1, 26)],
    26: [(-1, 25)],
    25: [(-1, 24)],
}
ROUNDS = [
    ([1, 16], [1, 16]),
    ([2, 15, 32], [2, 15]),
    ([3, 14, 31], [3, 14]),
    ([17], [17, 31]),
    ([4, 13, 30], [4, 13]),
    ([18], [18, 30]),
    ([5, 12, 29], [5, 12]),
    ([19], [19, 29]),
    ([6, 11, 28], [6, 11]),
    ([20], [20, 28]),
    ([7, 10, 27], [7, 10]),
    ([21], [21, 27]),
    ([9, 26], [9]),
    ([22], [22, 26]),
    ([8, 25], [8]),
    ([23], [23, 25]),
    ([24], [24, 32]),
]
SINKS_AFTER = 14
SHIFTS = sorted({shift % NS for moves in ONWARD.values() for shift, _ in moves} | {32, 48})
SLOT = {0: 0}
for _, group in ROUNDS:
    for j in group:
        SLOT[j] = len(SLOT)


def block_copies(buf, cs, cr):
    s, t, x, c, y, z = coords()

    def copy(kv, j, shift, there):
        src, dst = buf.at[SLOT[j], kv], buf.at[SLOT[there], kv]
        return remote(src, dst, cs.at[kv, there], cr.at[kv, there], lax.rem(s + shift + NS, NS), t)

    def forward(kv, j):
        for shift, there in ONWARD.get(j, []):
            copy(kv, j, shift, there).start()

    return copy, forward


def attention(
    copy, forward, q_ref, i_ref, o_ref,
    buf, acc, m_ref, l_ref, column, sacc_k, sacc_v, out_k, out_v, in_k, in_v, more_k, more_v, ss, sr,
):
    s, t, x, c, y, z = coords()

    def at(shift):
        return lax.rem(s + shift + NS, NS)

    sink_row = i_ref[...]
    for i in range(NSINK // TQ):
        part = jnp.broadcast_to(sink_row[:, i * TQ : (i + 1) * TQ], (TQ, TQ)).astype(F32)
        column[i] = jnp.transpose(part)

    scale = HD ** (-0.5)
    k_row = lax.broadcasted_iota(jnp.int32, (TQ, TQ), 0)
    q_col = lax.broadcasted_iota(jnp.int32, (TQ, TQ), 1)

    def attend(keys, values, masks, first=False):
        n = len(masks)
        for g in range(G):
            cols = slice(g * TQ, (g + 1) * TQ)
            scores = jnp.dot(keys(), q_ref[:, cols], preferred_element_type=F32)
            tiles = []
            for i, mask in enumerate(masks):
                tile = scores[i * TQ : (i + 1) * TQ]
                tiles.append(tile if mask is None else jnp.where(mask(), tile, -1e30))
            scores = jnp.concatenate(tiles, axis=0).reshape(n * TQ // 8, 8, TQ)
            top = jnp.max(jnp.max(scores, axis=0), axis=0, keepdims=True) * scale
            top = jnp.broadcast_to(top, (8, TQ))
            if not first:
                old = m_ref[:, cols]
                top = jnp.maximum(old, top)
                factor = jnp.exp(old - top)
            m_ref[:, cols] = top
            weights = jnp.exp(scores * scale - top[None])
            summed = jnp.sum(weights, axis=0)
            out = jnp.dot(values(), weights.reshape(n * TQ, TQ).astype(BF), preferred_element_type=F32)
            if first:
                l_ref[:, cols] = summed
                acc[:, cols] = out
            else:
                l_ref[:, cols] = l_ref[:, cols] * factor + summed
                scaled = acc[:, cols].reshape(HD // 8, 8, TQ) * factor[None]
                acc[:, cols] = scaled.reshape(HD, TQ) + out

    def attend_blocks(group, masks, first=False):
        start, n = SLOT[group[0]], len(group)
        attend(
            lambda: buf[start : start + n, 0].reshape(n * TQ, HD),
            lambda: jnp.concatenate([buf[start + i, 1] for i in range(n)], axis=1),
            masks,
            first,
        )

    def mask_of(j, guard):
        if j == 32:
            return lambda: (k_row > q_col) & (s >= 32)
        return (lambda: jnp.broadcast_to(s >= j, (TQ, TQ))) if guard else None

    def group_attend(group):
        @pl.when(s >= max(group))
        def _():
            attend_blocks(group, [mask_of(j, False) for j in group])

        @pl.when((s >= min(group)) & (s < max(group)))
        def _():
            attend_blocks(group, [mask_of(j, True) for j in group])

    def extract(j):
        base = (s - j) * TQ
        token = (q_col + base).astype(F32)
        hot = jnp.concatenate(
            [jnp.where(column[i] == token, 1.0, 0.0).astype(BF) for i in range(NSINK // TQ)], axis=0
        )
        k_part = jnp.dot(hot, buf[SLOT[j], 0], preferred_element_type=F32)
        across = jnp.broadcast_to(sink_row, (TQ, NSINK)) - base
        hot = jnp.where(across == lax.broadcasted_iota(jnp.int32, (TQ, NSINK), 0), 1.0, 0.0).astype(BF)
        v_part = jnp.dot(buf[SLOT[j], 1], hot, preferred_element_type=F32)
        if j == 0:
            sacc_k[...] = k_part
            sacc_v[...] = v_part
        else:
            sacc_k[...] += k_part
            sacc_v[...] += v_part

    attend_blocks([0], [lambda: k_row <= q_col], first=True)

    @pl.when(y < 2)
    def _():
        extract(0)

    def sink_copies(more, n, shift):
        dst_k, dst_v = (more_k, more_v) if more else (in_k, in_v)
        return (
            remote(out_k, dst_k, ss.at[n, 0], sr.at[n, 0], at(shift), t),
            remote(out_v, dst_v, ss.at[n, 1], sr.at[n, 1], at(shift), t),
        )

    for index, (waits, group) in enumerate(ROUNDS):
        for kv in range(2):
            for j in waits:
                copy(kv, j, 1, j).wait_recv()
                forward(kv, j)
        group_attend(group)
        for j in group:
            if j < 16:
                @pl.when((y < 2) & (s >= j))
                def _(j=j):
                    extract(j)
        if index == SINKS_AFTER:
            @pl.when(y < 2)
            def _():
                out_k[...] = sacc_k[...].astype(BF)
                out_v[...] = sacc_v[...].astype(BF)

            @pl.when(y == 0)
            def _():
                for one in sink_copies(False, 1, 48) + sink_copies(False, 0, 32):
                    one.start()

            @pl.when(y == 1)
            def _():
                for one in sink_copies(True, 2, 32):
                    one.start()

    @pl.when(y == 2)
    def _():
        for one in sink_copies(False, 0, 32):
            one.wait_recv()

    @pl.when(y == 3)
    def _():
        for one in sink_copies(False, 1, 48) + sink_copies(True, 2, 32):
            one.wait_recv()
        in_k[...] = in_k[...] + more_k[...]
        in_v[...] = in_v[...] + more_v[...]

    @pl.when(y >= 2)
    def _():
        limit = (q_col + (s * TQ - W)).astype(F32)
        attend(
            lambda: in_k[...],
            lambda: in_v[...],
            [lambda i=i: column[i] <= limit for i in range(NSINK // TQ)],
        )

    for g in range(G):
        cols = slice(g * TQ, (g + 1) * TQ)
        total = jnp.sum(l_ref[:, cols], axis=0, keepdims=True)
        o_ref[:, cols] = jnp.transpose(acc[:, cols] / total).astype(BF)

    for j, moves in ONWARD.items():
        for shift, there in moves:
            for kv in range(2):
                copy(kv, j, shift, there).wait_send()

    @pl.when(y == 0)
    def _():
        for one in sink_copies(False, 1, 48) + sink_copies(False, 0, 32):
            one.wait_send()

    @pl.when(y == 1)
    def _():
        for one in sink_copies(True, 2, 32):
            one.wait_send()


def local(queries, hidden, key_value_weight, key_value_bias, positions, sink_index):
    vmem = pl.BlockSpec(memory_space=pltpu.VMEM)
    hbm = pl.BlockSpec(memory_space=pl.ANY)
    dma = pltpu.SemaphoreType.DMA
    keys = W + TQ + NSINK
    shared = [
        pltpu.VMEM((HD, G * TQ), BF),
        pltpu.VMEM((33, 2, TQ, HD), BF),
        pltpu.VMEM((1, NSINK), jnp.int32),
        dma((2, 33)),
        dma((2, 33)),
    ]
    projecting = [
        pltpu.VMEM((TQ, G * HD), BF),
        pltpu.VMEM((2, HD), BF),
        pltpu.VMEM((3, TQ), jnp.int32),
        pltpu.VMEM((NY, TQ, DL), BF),
        pltpu.VMEM((2, 8, 2, 16, DL), BF),
        pltpu.VMEM((2, NY, TQ, HD), F32),
        pltpu.VMEM((2, NY, TQ, HD), F32),
        pltpu.VMEM((2, NY, TQ, HD), F32),
        pltpu.VMEM((2, NX, TQ, HD), F32),
        pltpu.VMEM((16, TQ), F32),
        pltpu.VMEM((16, HD), F32),
        pltpu.VMEM((2, TQ, HD), BF),
        dma((6,)),
        dma((NY,)),
        dma((NY,)),
        dma((2, NZ)),
        dma((2, NZ)),
        dma((2, NY)),
        dma((2, NY)),
        dma((2, NX)),
        dma((2, NX)),
        dma((2, NY)),
        dma((2,)),
        dma((2,)),
        dma((2,)),
    ]
    attending = [
        pltpu.VMEM((HD, G * TQ), F32),
        pltpu.VMEM((8, G * TQ), F32),
        pltpu.VMEM((8, G * TQ), F32),
        pltpu.VMEM((NSINK // TQ, TQ, TQ), F32),
        pltpu.VMEM((NSINK, HD), F32),
        pltpu.VMEM((HD, NSINK), F32),
    ]
    attending += [pltpu.VMEM((NSINK, HD), BF), pltpu.VMEM((HD, NSINK), BF)] * 3
    attending += [dma((3, 2)), dma((3, 2))]

    def whole(*refs):
        inputs, o_ref, refs = refs[:6], refs[6], refs[7:]
        (turned, buf, sinks), refs = refs[:3], refs[3:]
        (cs, cr), refs = refs[:2], refs[2:]
        copy, forward = block_copies(buf, cs, cr)
        finish = project(forward, *inputs, turned, buf.at[0], sinks, *refs[: len(projecting)])
        attention(copy, forward, turned, sinks, o_ref, buf, *refs[len(projecting) :])
        finish()

    return pl.pallas_call(
        whole,
        out_shape=jax.ShapeDtypeStruct((TQ, G * HD), BF),
        in_specs=[hbm] * 6,
        out_specs=vmem,
        scratch_shapes=shared + projecting + attending,
        compiler_params=pltpu.CompilerParams(
            collective_id=0, has_side_effects=True, vmem_limit_bytes=56 * 2**20
        ),
        cost_estimate=pl.CostEstimate(
            flops=4 * G * TQ * keys * HD + 2 * 512 * 512 * DL,
            bytes_accessed=2**20,
            transcendentals=G * TQ * keys,
        ),
        name="windowed",
    )(
        queries,
        hidden,
        jnp.swapaxes(key_value_weight, 1, 2),
        key_value_bias,
        positions,
        sink_index.reshape(1, NSINK),
    )


def solution(mesh):
    placed = (
        P("seq", "tensor"),
        P("seq", "tensor"),
        P(None, "tensor", "seq"),
        P(None, "tensor"),
        P(None, "seq"),
        P(),
    )
    return jax.shard_map(
        local, mesh=mesh, in_specs=placed, out_specs=P("seq", "tensor"), check_vma=False
    )
```

```python
import functools
import math

import jax
import jax.numpy as jnp
from jax import lax
from jax.experimental import pallas as pl
from jax.experimental.pallas import tpu as pltpu
from jax.sharding import PartitionSpec as P

H = 64
KVH = 8
HD = 128
W = 4096
NX = 4
NY = 4
NZ = 16
NS = NY * NZ
TQ = 128
G = H // KVH
DL = 1024
NSINK = 512
MESH = pl.DeviceIdType.MESH
LOG2E = 1.4426950408889634
BF = jnp.bfloat16
F32 = jnp.float32


def coords():
    s = lax.axis_index("seq")
    t = lax.axis_index("tensor")
    return s, t, t // 2, t % 2, s // NZ, s % NZ


def remote(src, dst, send, recv, seq, tensor):
    return pltpu.make_async_remote_copy(
        src_ref=src,
        dst_ref=dst,
        send_sem=send,
        recv_sem=recv,
        device_id=(seq, tensor),
        device_id_type=MESH,
    )


def nt_dot(a, b):
    return lax.dot_general(a, b, (((1,), (1,)), ((), ())), preferred_element_type=F32)


def rope_tables(pos):
    half = HD // 2
    pair = lax.broadcasted_iota(jnp.int32, (half, TQ), 0)
    inverse = jnp.exp(pair.astype(F32) * (-2.0 * math.log(1000000.0) / HD))
    first = HD // 8
    second = first + 3 * HD // 16
    temporal, height, width = (jnp.broadcast_to(pos[i : i + 1], (half, TQ)) for i in range(3))
    chosen = jnp.where(pair < first, temporal, jnp.where(pair < second, height, width))
    angles = chosen * inverse
    return jnp.cos(angles), jnp.sin(angles)


def rotate(u, tables):
    cosine, sine = tables
    top, low = u[: HD // 2], u[HD // 2 :]
    return jnp.concatenate([top * cosine - low * sine, low * cosine + top * sine], axis=0)


W_ONWARD = {
    0: [1, -1, 2, -2],
    1: [2], 2: [2], 3: [2], 4: [2], 5: [2], 6: [2],
    15: [-2], 14: [-2], 13: [-2], 12: [-2], 11: [-2],
}
W_ROUNDS = [[1, 15, 2, 14], [3, 13, 4, 12], [5, 11, 6, 10], [7, 9, 8]]


def project(
    forward, q_hbm, h_hbm, w_hbm, b_hbm, p_hbm, i_hbm, qo_ref, first_block, sinks,
    q_ref, b_ref, p_ref, hid, wbuf, p3s, p3r, p4s, p4r, pos, bias, kvs,
    ins, hs, hr, ws, wr, p3ss, p3rs, p4ss, p4rs, ps, pr, ts, tr,
):
    s, t, x, c, y, z = coords()
    other = x * 2 + (1 - c)
    mine = x == y

    def on_z(d):
        return y * NZ + lax.rem(z + d + NZ, NZ)

    def on_y(d):
        return lax.rem(y + d, NY) * NZ + z

    def on_x(d):
        return lax.rem(x + d, NX) * 2 + c

    barrier = pltpu.get_barrier_semaphore()

    def greet(seq, tensor):
        pl.semaphore_signal(barrier, inc=1, device_id=(seq, tensor), device_id_type=MESH)

    own_w = wbuf.at[z // 8, lax.rem(z, 8)]
    loads = [
        pltpu.make_async_copy(src, dst, ins.at[i])
        for i, (src, dst) in enumerate(
            [(w_hbm, own_w), (h_hbm, hid.at[y]), (p_hbm, p_ref), (b_hbm, b_ref), (q_hbm, q_ref), (i_hbm, sinks)]
        )
    ]
    for load in loads:
        load.start()
    greet(s, other)
    for shift in SHIFTS:
        greet(lax.rem(s - shift + NS, NS), t)
    for d in (1, -1, 2, -2):
        greet(on_z(d), t)
    for d in range(1, NY):
        greet(on_y(d), t)
        greet(s, on_x(d))

    @pl.when(jnp.logical_not(mine))
    def _():
        greet(x * NZ + z, y * 2 + c)

    pl.semaphore_wait(barrier, jnp.where(mine, 11, 12) + len(SHIFTS))
    loads[0].wait()

    def w_block(d):
        origin = lax.rem(z - d + NZ, NZ)
        return wbuf.at[origin // 8, lax.rem(origin, 8)]

    def w_copy(kv, d, hop):
        there = (d + hop) % NZ
        block = w_block(d).at[kv]
        return remote(block, block, ws.at[kv, there], wr.at[kv, there], on_z(hop), t)

    def w_forward(kv, d):
        for hop in W_ONWARD.get(d, []):
            w_copy(kv, d, hop).start()

    def w_wait(kv, d):
        block = w_block(d).at[kv]
        remote(block, block, ws.at[kv, d], wr.at[kv, d], s, t).wait_recv()

    for kv in range(2):
        w_forward(kv, 0)

    def h_copy(d):
        return remote(hid.at[y], hid.at[y], hs.at[d], hr.at[d], on_y(d), t)

    loads[1].wait()
    for d in (1, 3, 2):
        h_copy(d).start()
    for load in loads[2:]:
        load.wait()
    pos[0:3] = p_ref[...].astype(F32)
    pos[3:8] = jnp.zeros((5, TQ), F32)
    bias[0:2] = b_ref[...].astype(F32)
    bias[2:8] = jnp.zeros((6, HD), F32)

    def p_copy(d):
        return remote(pos.at[pl.ds(0, 8)], pos.at[pl.ds(8, 8)], ps.at[0, d], pr.at[0], on_y(d), t)

    def b_copy(d):
        return remote(bias.at[pl.ds(0, 8)], bias.at[pl.ds(8, 8)], ps.at[1, d], pr.at[1], s, on_x(d))

    @pl.when(mine)
    def _():
        pos[8:16] = pos[0:8]
        bias[8:16] = bias[0:8]
        for d in range(1, NY):
            p_copy(d).start()
            b_copy(d).start()

    own_tables = rope_tables(pos[0:8])

    def turn_query(g):
        u = jnp.transpose(q_ref[:, g * HD : (g + 1) * HD].astype(F32))
        qo_ref[:, g * TQ : (g + 1) * TQ] = rotate(u, own_tables).astype(BF)

    for index, arrived in enumerate(W_ROUNDS[:-1]):
        for kv in range(2):
            for d in arrived:
                w_wait(kv, d)
                w_forward(kv, d)
        share = -(-G // (len(W_ROUNDS) - 1))
        for g in range(index * share, min((index + 1) * share, G)):
            turn_query(g)

    @pl.when(jnp.logical_not(mine))
    def _():
        p_copy(1).wait_recv()
        b_copy(1).wait_recv()

    tables = rope_tables(pos[8:16])
    for d in range(1, NY):
        slot = hid.at[lax.rem(y + NY - d, NY)]
        remote(slot, slot, hs.at[d], hr.at[d], s, t).wait_recv()

    def product(kv, head, out):
        rows = hid[...].reshape(NY * TQ, DL)
        cols = wbuf[head, :, kv].reshape(HD, DL)
        part = nt_dot(rows, cols).reshape(NY, TQ, HD)
        for i in range(NY):
            out[kv, i] = part[i]

    def p3_copy(kv, i):
        return remote(p3s.at[kv, i], p3r.at[kv, i], p3ss.at[kv, i], p3rs.at[kv, i], s, other)

    def p4_copy(kv, i):
        return remote(p4s.at[kv, i], p4r.at[kv, x], p4ss.at[kv, i], p4rs.at[kv, x], s, i * 2 + c)

    for kv in range(2):
        for d in W_ROUNDS[-1]:
            w_wait(kv, d)
        product(kv, 1 - c, p3s)
        for i in range(NY):
            p3_copy(kv, i).start()
        product(kv, c, p4s)

    for kv in range(2):
        for i in range(NY):
            p3_copy(kv, i).wait_recv()
            p4s[kv, i] += p3r[kv, i]

            @pl.when(x == i)
            def _(kv=kv, i=i):
                p4r[kv, x] = p4s[kv, i]

            @pl.when(x != i)
            def _(kv=kv, i=i):
                p4_copy(kv, i).start()

    def t_copy(kv):
        return remote(kvs.at[kv], first_block.at[kv], ts.at[kv], tr.at[kv], x * NZ + z, y * 2 + c)

    for kv in range(2):
        for i in range(NX):
            @pl.when(x != i)
            def _(kv=kv, i=i):
                slot = p4r.at[kv, i]
                remote(slot, slot, p4ss.at[kv, i], p4rs.at[kv, i], s, t).wait_recv()

        total = (p4r[kv, 0] + p4r[kv, 1]) + (p4r[kv, 2] + p4r[kv, 3]) + bias[8 + kv : 9 + kv]
        total = jnp.transpose(total)
        if kv == 0:
            total = jnp.transpose(rotate(total, tables))
        kvs[kv] = total.astype(BF)

        @pl.when(mine)
        def _(kv=kv):
            first_block[kv] = kvs[kv]

        @pl.when(jnp.logical_not(mine))
        def _(kv=kv):
            t_copy(kv).start()

    for kv in range(2):
        @pl.when(jnp.logical_not(mine))
        def _(kv=kv):
            t_copy(kv).wait_recv()

        forward(kv, 0)

    def finish():
        for d, hops in W_ONWARD.items():
            for hop in hops:
                for kv in range(2):
                    w_copy(kv, d, hop).wait_send()
        for d in range(1, NY):
            h_copy(d).wait_send()
        for kv in range(2):
            for i in range(NY):
                p3_copy(kv, i).wait_send()

                @pl.when(x != i)
                def _(kv=kv, i=i):
                    p4_copy(kv, i).wait_send()

        @pl.when(mine)
        def _():
            for d in range(1, NY):
                p_copy(d).wait_send()
                b_copy(d).wait_send()

        @pl.when(jnp.logical_not(mine))
        def _():
            for kv in range(2):
                t_copy(kv).wait_send()

    return finish


ONWARD = {
    0: [(1, 1), (16, 16), (32, 32)],
    16: [(-1, 15)],
    32: [(-1, 31)],
    1: [(1, 2), (16, 17)],
    2: [(1, 3), (16, 18)],
    3: [(1, 4), (16, 19)],
    4: [(1, 5), (16, 20)],
    5: [(1, 6), (16, 21)],
    6: [(1, 7), (16, 22)],
    7: [(16, 23)],
    15: [(-1, 14)],
    14: [(-1, 13)],
    13: [(-1, 12)],
    12: [(-1, 11)],
    11: [(-1, 10)],
    10: [(-1, 9)],
    9: [(-1, 8)],
    31: [(-1, 30)],
    30: [(-1, 29)],
    29: [(-1, 28)],
    28: [(-1, 27)],
    27: [(-1, 26)],
    26: [(-1, 25)],
    25: [(-1, 24)],
}
ROUNDS = [
    ([1, 16], [1, 16]),
    ([2, 15, 32], [2, 15]),
    ([3, 14, 31], [3, 14]),
    ([17], [17, 31, 32]),
    ([4, 13, 30], [4, 13]),
    ([18], [18, 30]),
    ([5, 12, 29], [5, 12]),
    ([19], [19, 29]),
    ([6, 11, 28], [6, 11]),
    ([20], [20, 28]),
    ([7, 10, 27], [7, 10]),
    ([21], [21, 27]),
    ([9, 26], [9]),
    ([22], [22, 26]),
    ([8, 25], [8]),
    ([23], [23, 25]),
    ([24], [24]),
]
SINKS_AFTER = 14
SHIFTS = sorted({shift % NS for moves in ONWARD.values() for shift, _ in moves} | {32, 48})
SLOT = {0: 0}
for _, group in ROUNDS:
    for j in group:
        SLOT[j] = len(SLOT)


def block_copies(buf, cs, cr):
    s, t, x, c, y, z = coords()

    def copy(kv, j, shift, there):
        src, dst = buf.at[SLOT[j], kv], buf.at[SLOT[there], kv]
        return remote(src, dst, cs.at[kv, there], cr.at[kv, there], lax.rem(s + shift + NS, NS), t)

    def forward(kv, j):
        for shift, there in ONWARD.get(j, []):
            copy(kv, j, shift, there).start()

    return copy, forward


def attention(
    copy, forward, q_ref, i_ref, o_ref,
    buf, acc, m_ref, l_ref, column, sacc_k, sacc_v, out_k, out_v, in_k, in_v, more_k, more_v, ss, sr,
):
    s, t, x, c, y, z = coords()

    def at(shift):
        return lax.rem(s + shift + NS, NS)

    sink_row = i_ref[...]
    for i in range(NSINK // TQ):
        part = jnp.broadcast_to(sink_row[:, i * TQ : (i + 1) * TQ], (TQ, TQ)).astype(F32)
        column[i] = jnp.transpose(part)

    scale = HD ** (-0.5)
    k_row = lax.broadcasted_iota(jnp.int32, (TQ, TQ), 0)
    q_col = lax.broadcasted_iota(jnp.int32, (TQ, TQ), 1)

    def attend(keys, values, masks, first=False):
        n = len(masks)
        for g in range(G):
            cols = slice(g * TQ, (g + 1) * TQ)
            scores = jnp.dot(keys(), q_ref[:, cols], preferred_element_type=F32)
            tiles = []
            for i, mask in enumerate(masks):
                tile = scores[i * TQ : (i + 1) * TQ]
                tiles.append(tile if mask is None else jnp.where(mask(), tile, -1e30))
            scores = jnp.concatenate(tiles, axis=0).reshape(n * TQ // 8, 8, TQ)
            top = jnp.max(jnp.max(scores, axis=0), axis=0, keepdims=True) * scale
            top = jnp.broadcast_to(top, (8, TQ))
            if not first:
                old = m_ref[:, cols]
                top = jnp.maximum(old, top)
                factor = jnp.exp(old - top)
            m_ref[:, cols] = top
            weights = jnp.exp(scores * scale - top[None])
            summed = jnp.sum(weights, axis=0)
            out = jnp.dot(values(), weights.reshape(n * TQ, TQ).astype(BF), preferred_element_type=F32)
            if first:
                l_ref[:, cols] = summed
                acc[:, cols] = out
            else:
                l_ref[:, cols] = l_ref[:, cols] * factor + summed
                scaled = acc[:, cols].reshape(HD // 8, 8, TQ) * factor[None]
                acc[:, cols] = scaled.reshape(HD, TQ) + out

    def attend_blocks(group, masks, first=False):
        start, n = SLOT[group[0]], len(group)
        attend(
            lambda: buf[start : start + n, 0].reshape(n * TQ, HD),
            lambda: jnp.concatenate([buf[start + i, 1] for i in range(n)], axis=1),
            masks,
            first,
        )

    def mask_of(j, guard):
        if j == 32:
            return lambda: (k_row > q_col) & (s >= 32)
        return (lambda: jnp.broadcast_to(s >= j, (TQ, TQ))) if guard else None

    def group_attend(group):
        @pl.when(s >= max(group))
        def _():
            attend_blocks(group, [mask_of(j, False) for j in group])

        @pl.when((s >= min(group)) & (s < max(group)))
        def _():
            attend_blocks(group, [mask_of(j, True) for j in group])

    def extract(j):
        base = (s - j) * TQ
        token = (q_col + base).astype(F32)
        hot = jnp.concatenate(
            [jnp.where(column[i] == token, 1.0, 0.0).astype(BF) for i in range(NSINK // TQ)], axis=0
        )
        k_part = jnp.dot(hot, buf[SLOT[j], 0], preferred_element_type=F32)
        across = jnp.broadcast_to(sink_row, (TQ, NSINK)) - base
        hot = jnp.where(across == lax.broadcasted_iota(jnp.int32, (TQ, NSINK), 0), 1.0, 0.0).astype(BF)
        v_part = jnp.dot(buf[SLOT[j], 1], hot, preferred_element_type=F32)
        if j == 0:
            sacc_k[...] = k_part
            sacc_v[...] = v_part
        else:
            sacc_k[...] += k_part
            sacc_v[...] += v_part

    attend_blocks([0], [lambda: k_row <= q_col], first=True)

    @pl.when(y < 2)
    def _():
        extract(0)

    def sink_copies(more, n, shift):
        dst_k, dst_v = (more_k, more_v) if more else (in_k, in_v)
        return (
            remote(out_k, dst_k, ss.at[n, 0], sr.at[n, 0], at(shift), t),
            remote(out_v, dst_v, ss.at[n, 1], sr.at[n, 1], at(shift), t),
        )

    for index, (waits, group) in enumerate(ROUNDS):
        for kv in range(2):
            for j in waits:
                copy(kv, j, 1, j).wait_recv()
                forward(kv, j)
        group_attend(group)
        for j in group:
            if j < 16:
                @pl.when((y < 2) & (s >= j))
                def _(j=j):
                    extract(j)
        if index == SINKS_AFTER:
            @pl.when(y < 2)
            def _():
                out_k[...] = sacc_k[...].astype(BF)
                out_v[...] = sacc_v[...].astype(BF)

            @pl.when(y == 0)
            def _():
                for one in sink_copies(False, 1, 48) + sink_copies(False, 0, 32):
                    one.start()

            @pl.when(y == 1)
            def _():
                for one in sink_copies(True, 2, 32):
                    one.start()

    @pl.when(y == 2)
    def _():
        for one in sink_copies(False, 0, 32):
            one.wait_recv()

    @pl.when(y == 3)
    def _():
        for one in sink_copies(False, 1, 48) + sink_copies(True, 2, 32):
            one.wait_recv()
        in_k[...] = in_k[...] + more_k[...]
        in_v[...] = in_v[...] + more_v[...]

    @pl.when(y >= 2)
    def _():
        limit = (q_col + (s * TQ - W)).astype(F32)
        attend(
            lambda: in_k[...],
            lambda: in_v[...],
            [lambda i=i: column[i] <= limit for i in range(NSINK // TQ)],
        )

    for g in range(G):
        cols = slice(g * TQ, (g + 1) * TQ)
        total = jnp.sum(l_ref[:, cols], axis=0, keepdims=True)
        o_ref[:, cols] = jnp.transpose(acc[:, cols] / total).astype(BF)

    for j, moves in ONWARD.items():
        for shift, there in moves:
            for kv in range(2):
                copy(kv, j, shift, there).wait_send()

    @pl.when(y == 0)
    def _():
        for one in sink_copies(False, 1, 48) + sink_copies(False, 0, 32):
            one.wait_send()

    @pl.when(y == 1)
    def _():
        for one in sink_copies(True, 2, 32):
            one.wait_send()


def local(queries, hidden, key_value_weight, key_value_bias, positions, sink_index):
    vmem = pl.BlockSpec(memory_space=pltpu.VMEM)
    hbm = pl.BlockSpec(memory_space=pl.ANY)
    dma = pltpu.SemaphoreType.DMA
    keys = W + TQ + NSINK
    shared = [
        pltpu.VMEM((HD, G * TQ), BF),
        pltpu.VMEM((33, 2, TQ, HD), BF),
        pltpu.VMEM((1, NSINK), jnp.int32),
        dma((2, 33)),
        dma((2, 33)),
    ]
    projecting = [
        pltpu.VMEM((TQ, G * HD), BF),
        pltpu.VMEM((2, HD), BF),
        pltpu.VMEM((3, TQ), jnp.int32),
        pltpu.VMEM((NY, TQ, DL), BF),
        pltpu.VMEM((2, 8, 2, 16, DL), BF),
        pltpu.VMEM((2, NY, TQ, HD), F32),
        pltpu.VMEM((2, NY, TQ, HD), F32),
        pltpu.VMEM((2, NY, TQ, HD), F32),
        pltpu.VMEM((2, NX, TQ, HD), F32),
        pltpu.VMEM((16, TQ), F32),
        pltpu.VMEM((16, HD), F32),
        pltpu.VMEM((2, TQ, HD), BF),
        dma((6,)),
        dma((NY,)),
        dma((NY,)),
        dma((2, NZ)),
        dma((2, NZ)),
        dma((2, NY)),
        dma((2, NY)),
        dma((2, NX)),
        dma((2, NX)),
        dma((2, NY)),
        dma((2,)),
        dma((2,)),
        dma((2,)),
    ]
    attending = [
        pltpu.VMEM((HD, G * TQ), F32),
        pltpu.VMEM((8, G * TQ), F32),
        pltpu.VMEM((8, G * TQ), F32),
        pltpu.VMEM((NSINK // TQ, TQ, TQ), F32),
        pltpu.VMEM((NSINK, HD), F32),
        pltpu.VMEM((HD, NSINK), F32),
    ]
    attending += [pltpu.VMEM((NSINK, HD), BF), pltpu.VMEM((HD, NSINK), BF)] * 3
    attending += [dma((3, 2)), dma((3, 2))]

    def whole(*refs):
        inputs, o_ref, refs = refs[:6], refs[6], refs[7:]
        (turned, buf, sinks), refs = refs[:3], refs[3:]
        (cs, cr), refs = refs[:2], refs[2:]
        copy, forward = block_copies(buf, cs, cr)
        finish = project(forward, *inputs, turned, buf.at[0], sinks, *refs[: len(projecting)])
        attention(copy, forward, turned, sinks, o_ref, buf, *refs[len(projecting) :])
        finish()

    return pl.pallas_call(
        whole,
        out_shape=jax.ShapeDtypeStruct((TQ, G * HD), BF),
        in_specs=[hbm] * 6,
        out_specs=vmem,
        scratch_shapes=shared + projecting + attending,
        compiler_params=pltpu.CompilerParams(
            collective_id=0, has_side_effects=True, vmem_limit_bytes=56 * 2**20
        ),
        cost_estimate=pl.CostEstimate(
            flops=4 * G * TQ * keys * HD + 2 * 512 * 512 * DL,
            bytes_accessed=2**20,
            transcendentals=G * TQ * keys,
        ),
        name="windowed",
    )(
        queries,
        hidden,
        jnp.swapaxes(key_value_weight, 1, 2),
        key_value_bias,
        positions,
        sink_index.reshape(1, NSINK),
    )


def solution(mesh):
    placed = (
        P("seq", "tensor"),
        P("seq", "tensor"),
        P(None, "tensor", "seq"),
        P(None, "tensor"),
        P(None, "seq"),
        P(),
    )
    return jax.shard_map(
        local, mesh=mesh, in_specs=placed, out_specs=P("seq", "tensor"), check_vma=False
    )
```
